512 devices in a mesh: ctx: 32 (over x, z_lo, core), tp: 16 (over z_hi, y).
Axes of the slice: x: 4, y: 4, z: 16 (z_hi: 4, z_lo: 4; z = z_hi * 4 + z_lo), core: 2. Of those that a mesh axis runs over, the one named last changes fastest.
Arguments:
- inputs: bfloat16 [3, 8192, 4096], P(None, 'tp', 'ctx'), may hold values from -6 to 6
- short_filters: float32 [3, 3, 8192], P(None, None, 'tp'), may hold values from -3 to 3
- explicit_filter: bfloat16 [512, 128], P('tp'), may hold values from -0.81 to 0.81
- skip_gain: float32 [8192], P('tp'), may hold values from 0.5 to 1.5
- out_weight: bfloat16 [8192, 8192], P('tp', 'ctx'), may hold values from -0.125 to 0.125
- out_cotangent: bfloat16 [8192, 4096], P('tp', 'ctx'), may hold values from -6 to 6
Outputs:
- output: bfloat16 [8192, 4096], P('tp', 'ctx')
- grad_inputs: bfloat16 [3, 8192, 4096], P(None, 'tp', 'ctx')
- grad_filter: float32 [512, 128], P('tp')
- grad_skip: float32 [8192], P('tp')
The draws below stay inside these ranges and needn't reach their ends.
All inputs are finite; a program needn't handle non-finite values.
Results may differ from the reference program's by a relative error of at most 0.0059.
Values may be sent and summed in bfloat16 or wider, within the bound.
A program may use at most 64 MiB of HBM per device.

```python
import math
import jax
import jax.numpy as jnp
from jax import lax

D = 8192
FILTER = 128
L = 4096
G = 512


def draw_explicit_filter(key, part):
    key = jax.random.fold_in(key, 7)
    rate_key, tap_key = jax.random.split(key)
    decay_rates = jnp.exp(jax.random.uniform(rate_key, (G, 1), jnp.float32, math.log(1.0 / 400.0), math.log(1.0 / 25.0)))
    tap_values = jnp.clip(jax.random.normal(tap_key, (G, FILTER), jnp.float32), -4.0, 4.0)
    envelope = jnp.exp(-decay_rates * jnp.arange(FILTER, dtype=jnp.float32)[None, :])
    return (0.2 * tap_values * envelope).astype(jnp.bfloat16)


def strengthened(values, rng, source, target, parts, factor):
    owner, partner = [(jnp.arange(values.shape[axis_at]) // (values.shape[axis_at] // parts)).reshape([-1 if axis == axis_at else 1 for axis in range(values.ndim)]) for axis_at in (source, target)]
    chosen = jax.random.permutation(rng, parts)[partner]
    strong = (owner == chosen) | (owner == (partner + parts // 2) % parts)
    return jnp.where(strong, factor * values, values)


def levels(rng, shape, cuts, least, high):
    def one(axis_at, parts):
        draws = jax.random.uniform(jax.random.fold_in(jax.random.fold_in(rng, 6), axis_at), (parts,), jnp.float32, least / len(cuts), high / len(cuts))
        return jnp.repeat(jnp.exp(draws), shape[axis_at] // parts).reshape((-1,) + (1,) * (len(shape) - axis_at - 1))

    level = one(*cuts[0])
    for cut in cuts[1:]:
        level = level * one(*cut)
    return level


def scatter_about(stream_key, extent, spread, reach, cuts=(), kind=jnp.bfloat16):
    level = levels(stream_key, extent, cuts, -0.22, 0.18) if cuts else 1.0
    array = jax.random.normal(stream_key, extent, jnp.float32) * spread * level
    return jnp.minimum(jnp.maximum(array, -reach), reach).astype(kind)


def noise_with(rng, extent, width, most, cuts, heavy, held_as=jnp.bfloat16):
    result = width * jax.random.normal(rng, extent, jnp.float32)
    if cuts:
        result = result * levels(rng, extent, cuts, -0.22, 0.18)
    return jnp.clip(strengthened(result, jax.random.fold_in(rng, 3), *heavy), -most, most).astype(held_as)


def setup_inputs(seed: int = 0) -> dict:
    keys = jax.random.split(jax.random.key(seed), 7)
    inputs = scatter_about(keys[0], (3, D, L), 1.0, 6.0, ((1, 16), (2, 32)))
    short_filters = scatter_about(keys[1], (3, 3, D), 0.5, 3.0, ((2, 16),), jnp.float32)
    explicit_filter = draw_explicit_filter(jax.random.fold_in(keys[6], 71), 0)
    skip_gain = jnp.clip(0.5 + 1.0 * jax.random.uniform(keys[3], (D,), jnp.float32) ** levels(keys[3], (D,), ((0, 16),), -0.2, 0.2), 0.5, 1.5)
    out_weight = noise_with(keys[4], (D, D), D ** -0.5, 0.125, ((0, 16), (1, 32)), (0, 1, 32, 2.75))
    out_cotangent = scatter_about(keys[5], (D, L), 1.0, 6.0, ((0, 16), (1, 32)))
    return dict(inputs=inputs, short_filters=short_filters, explicit_filter=explicit_filter, skip_gain=skip_gain, out_weight=out_weight, out_cotangent=out_cotangent)


HIGH = lax.Precision.HIGHEST


def toeplitz(filter_rows_in):
    block_len = filter_rows_in.shape[1]
    offset = jnp.arange(block_len)[None, :] - jnp.arange(block_len)[:, None]
    current = jnp.take(filter_rows_in, jnp.where(offset >= 0, offset, 0), axis=1)
    current = jnp.where(offset >= 0, current, jnp.zeros_like(current))
    previous = jnp.take(filter_rows_in, jnp.where(offset < 0, offset + block_len, 0), axis=1)
    previous = jnp.where(offset < 0, previous, jnp.zeros_like(previous))
    return current, previous


def diagonals(matrix):
    amount = matrix.shape[0]
    block_len = matrix.shape[1]
    padded = jnp.pad(matrix, ((0, 0), (0, 0), (0, block_len)))
    flattened = jnp.pad(padded.reshape(amount, 2 * block_len * block_len), ((0, 0), (0, block_len)))
    skewed = flattened.reshape(amount, block_len, 2 * block_len + 1)[:, :, :block_len]
    return jnp.sum(skewed, axis=1)


def filter_terms(corr_now, corr_back):
    forward_part = diagonals(corr_now)
    backward_part = diagonals(corr_back)
    shifted = jnp.concatenate([jnp.zeros_like(backward_part[:, :1]), jnp.flip(backward_part[:, 1:], axis=1)], axis=1)
    return forward_part + shifted


def short_forward(padded, filters, length):
    summed = filters[:, 0, :, None] * padded[:, :, 2:2 + length]
    summed = summed + filters[:, 1, :, None] * padded[:, :, 1:1 + length]
    return summed + filters[:, 2, :, None] * padded[:, :, 0:length]


def short_backward(padded, filters, length):
    summed = filters[:, 0, :, None] * padded[:, :, 0:length]
    summed = summed + filters[:, 1, :, None] * padded[:, :, 1:1 + length]
    return summed + filters[:, 2, :, None] * padded[:, :, 2:2 + length]


def reference(inputs, short_filters, explicit_filter, skip_gain, out_weight, out_cotangent):
    channels = inputs.shape[1]
    length = inputs.shape[2]
    groups = explicit_filter.shape[0]
    block_len = explicit_filter.shape[1]
    per_group = channels // groups
    blocks = length // block_len
    padded = jnp.pad(inputs.astype(jnp.float32), ((0, 0), (0, 0), (2, 0)))
    features = short_forward(padded, short_filters, length)
    query_feat = features[0]
    key_feat = features[1]
    value_feat = features[2]
    product = lax.optimization_barrier((key_feat * value_feat).astype(jnp.bfloat16))
    product_f = product.astype(jnp.float32)
    current, previous = toeplitz(explicit_filter.astype(jnp.float32))
    stacked = product_f.reshape(groups, per_group, blocks, block_len)
    extended = jnp.concatenate([jnp.zeros((groups, per_group, 1, block_len), jnp.float32), stacked], axis=2)
    response = jnp.einsum('gcbs,gst->gcbt', extended[:, :, 1:], current, precision=HIGH)
    response = response + jnp.einsum('gcbs,gst->gcbt', extended[:, :, :-1], previous, precision=HIGH)
    response = response.reshape(channels, length) + skip_gain[:, None] * product_f
    gated = (query_feat * response).astype(jnp.bfloat16)
    output = lax.dot_general(out_weight, gated, (((0,), (0,)), ((), ())), preferred_element_type=jnp.float32).astype(jnp.bfloat16)
    grad_gated = lax.optimization_barrier(jnp.dot(out_weight, out_cotangent, preferred_element_type=jnp.float32).astype(jnp.bfloat16))
    grad_full = grad_gated.astype(jnp.float32)
    grad_query = grad_full * response
    grad_resp = lax.optimization_barrier((grad_full * query_feat).astype(jnp.bfloat16))
    grad_resp_f = grad_resp.astype(jnp.float32)
    grad_blocks = grad_resp_f.reshape(groups, per_group, blocks, block_len)
    grad_ext = jnp.concatenate([grad_blocks, jnp.zeros((groups, per_group, 1, block_len), jnp.float32)], axis=2)
    grad_prod = jnp.einsum('gcbt,gst->gcbs', grad_ext[:, :, :-1], current, precision=HIGH)
    grad_prod = grad_prod + jnp.einsum('gcbt,gst->gcbs', grad_ext[:, :, 1:], previous, precision=HIGH)
    grad_prod = grad_prod.reshape(channels, length) + skip_gain[:, None] * grad_resp_f
    corr_now = jnp.einsum('gcbs,gcbt->gst', extended[:, :, 1:], grad_blocks, precision=HIGH)
    corr_back = jnp.einsum('gcbs,gcbt->gts', extended[:, :, :-1], grad_blocks, precision=HIGH)
    grad_filter = filter_terms(corr_now, corr_back)
    grad_skip = jnp.sum(grad_resp_f * product_f, axis=1)
    grad_feat = jnp.stack([grad_query, grad_prod * value_feat, grad_prod * key_feat])
    back_pad = jnp.pad(grad_feat, ((0, 0), (0, 0), (0, 2)))
    grad_inputs = short_backward(back_pad, short_filters, length).astype(jnp.bfloat16)
    return output, grad_inputs, grad_filter, grad_skip
```

```python
import jax
import jax.numpy as jnp
from jax import lax
from jax.experimental import pallas as pl
from jax.experimental.pallas import tpu as pltpu
from jax.sharding import PartitionSpec as P

MESH = pl.DeviceIdType.MESH
BF = jnp.bfloat16
F32 = jnp.float32
N_SEND = 128
N_RECV = 128


def nt_dot(a, b):
    return lax.dot_general(a, b, (((1,), (1,)), ((), ())), preferred_element_type=F32)


def tn_dot(a, b):
    return lax.dot_general(a, b, (((0,), (0,)), ((), ())), preferred_element_type=F32)


def nn_dot(a, b):
    return jnp.dot(a, b, preferred_element_type=F32)


def kernel(
    inp, taps, filt, skip, w_hbm, cot_hbm,
    out, ginp, gfilt, gskip,
    wall, call, toep, coef, tail_out, tail_in, tail_cols, qf, kf, vf, prod, prev, resp, gated_t,
    acc, part, gout, gnext, gprod, gtail_out, gtail_in, gtail_cols,
    y_half, y_full, y_stage, z_half, z_full, z_stage, z_own,
    pay, pay_in, local_sem, ssem, rsem, wz_sem, wsib_sem,
):
    ctx, tp = lax.axis_index("ctx"), lax.axis_index("tp")
    x, zl, core = ctx // 8, (ctx // 2) % 4, ctx % 2
    zh, y = tp // 4, tp % 4

    def at_ctx(x_, zl_, core_):
        return ((x_ * 4 + zl_) * 2 + core_, tp)

    def at_tp(zh_, y_):
        return (ctx, zh_ * 4 + y_)

    def plus(v, d):
        return (v + d) % 4

    x_right, x_left, x_far = at_ctx(plus(x, 1), zl, core), at_ctx(plus(x, 3), zl, core), at_ctx(plus(x, 2), zl, core)
    l_up, l_down, l_far = at_ctx(x, plus(zl, 1), core), at_ctx(x, plus(zl, 3), core), at_ctx(x, plus(zl, 2), core)
    sibling = at_ctx(x, zl, 1 - core)
    later, earlier = ((ctx + 1) % 32, tp), ((ctx + 31) % 32, tp)
    h_right, h_left = at_tp(plus(zh, 1), y), at_tp(plus(zh, 3), y)
    y_right, y_left = at_tp(zh, plus(y, 1)), at_tp(zh, plus(y, 3))

    upper = zl // 2
    inner = zl + upper * (3 - 2 * zl)
    step_dir = 1 - 2 * upper
    z_in = at_ctx(x, zl + step_dir, core)
    z_out = at_ctx(x, (zl - step_dir + 4) % 4, core)

    def unmirror(v):
        return v + upper * (3 - 2 * v)

    line = [zl, unmirror(1 - inner), unmirror(2), unmirror(3)]

    own = x * 4 + zl
    copy_w = pltpu.make_async_copy(w_hbm, wall.at[own, core], local_sem.at[0])
    copy_c = pltpu.make_async_copy(cot_hbm, call.at[tp], local_sem.at[1])
    copy_w.start()
    copy_c.start()

    partners = [x_right, x_left, x_far, l_up, l_down, l_far, sibling, later, earlier, h_right, h_left, y_right, y_left]
    barrier = pltpu.get_barrier_semaphore()
    for who in partners:
        pl.semaphore_signal(barrier, inc=1, device_id=who, device_id_type=MESH)

    count = {"s": 0, "r": 0}
    sends = []

    def new_recv():
        count["r"] += 1
        return rsem.at[count["r"] - 1]

    def send(src, dst, sem, who, when=None):
        copy = pltpu.make_async_remote_copy(src, dst, ssem.at[count["s"]], sem, device_id=who, device_id_type=MESH)
        count["s"] += 1
        if when is None:
            copy.start()
        else:
            pl.when(when)(lambda: copy.start())
        sends.append((copy, when))

    def arrived(dst, sem):
        pltpu.make_async_remote_copy(dst, dst, ssem.at[0], sem, device_id=sibling, device_id_type=MESH).wait_recv()

    for a in range(3):
        turned = inp[a].astype(F32).T
        tail_out[2 * a:2 * a + 2, :] = turned[126:128, :]
    tail_out[6:8, :] = jnp.zeros((2, 512), F32)

    copy_w.wait()
    copy_c.wait()
    pl.semaphore_wait(barrier, len(partners))

    r_tail = new_recv()
    send(tail_out, tail_in, r_tail, later)

    x_sems = [[new_recv() for _ in range(4)] for _ in range(4)]

    def w_start(s):
        n = x * 4 + line[s]
        if s > 0:
            arrived(wall.at[n, core], wz_sem.at[line[s]])
        block = wall.at[n, core]
        if s == 0:
            send(block, block, wz_sem.at[line[s]], z_in)
            send(block, block, wz_sem.at[line[s]], z_out, inner == 1)
        elif s == 1:
            send(block, block, wz_sem.at[line[s]], z_in, inner == 1)
        else:
            send(block, block, wz_sem.at[line[s]], z_out, inner == 1)
        send(block, block, x_sems[s][0], x_right)
        send(block, block, x_sems[s][1], x_left)
        send(block, block, wsib_sem.at[4 * s], sibling)

    def w_near(s):
        n = plus(x, 3) * 4 + line[s]
        block = wall.at[n, core]
        arrived(block, x_sems[s][0])
        half = wall.at[n, core, pl.ds(0, 256), :]
        send(half, half, x_sems[s][2], x_right)
        send(block, block, wsib_sem.at[4 * s + 1], sibling)
        n = plus(x, 1) * 4 + line[s]
        block = wall.at[n, core]
        arrived(block, x_sems[s][1])
        half = wall.at[n, core, pl.ds(256, 256), :]
        send(half, half, x_sems[s][3], x_left)
        send(block, block, wsib_sem.at[4 * s + 2], sibling)

    def w_far(s):
        n = plus(x, 2) * 4 + line[s]
        arrived(wall.at[n, core, pl.ds(0, 256), :], x_sems[s][2])
        arrived(wall.at[n, core, pl.ds(256, 256), :], x_sems[s][3])
        block = wall.at[n, core]
        send(block, block, wsib_sem.at[4 * s + 3], sibling)

    def w_sibling(s):
        for i, d in enumerate((0, 3, 1, 2)):
            n = plus(x, d) * 4 + line[s]
            arrived(wall.at[n, 1 - core], wsib_sem.at[4 * s + i])

    c_zsems = [new_recv() for _ in range(4)]
    c_ysems = [[new_recv() for _ in range(4)] for _ in range(4)]
    lo, hi = pl.ds(0, 256), pl.ds(256, 256)

    def c_start():
        block = call.at[tp]
        send(block, block, c_zsems[0], h_right)
        send(block, block, c_zsems[1], h_left)
        c_ysend(0)

    def c_ysend(d):
        block = call.at[plus(zh, d) * 4 + y]
        send(block, block, c_ysems[d][0], y_right)
        send(block, block, c_ysems[d][1], y_left)

    def c_znear():
        n = plus(zh, 3) * 4 + y
        arrived(call.at[n], c_zsems[0])
        half = call.at[n, lo, :]
        send(half, half, c_zsems[2], h_right)
        n = plus(zh, 1) * 4 + y
        arrived(call.at[n], c_zsems[1])
        half = call.at[n, hi, :]
        send(half, half, c_zsems[3], h_left)
        c_ysend(3)
        c_ysend(1)

    def c_zfar():
        n = plus(zh, 2) * 4 + y
        arrived(call.at[n, lo, :], c_zsems[2])
        arrived(call.at[n, hi, :], c_zsems[3])
        c_ysend(2)

    def c_ynear(d):
        n = plus(zh, d) * 4 + plus(y, 3)
        arrived(call.at[n], c_ysems[d][0])
        half = call.at[n, lo, :]
        send(half, half, c_ysems[d][2], y_right)
        n = plus(zh, d) * 4 + plus(y, 1)
        arrived(call.at[n], c_ysems[d][1])
        half = call.at[n, hi, :]
        send(half, half, c_ysems[d][3], y_left)

    def c_yfar(d):
        n = plus(zh, d) * 4 + plus(y, 2)
        arrived(call.at[n, lo, :], c_ysems[d][2])
        arrived(call.at[n, hi, :], c_ysems[d][3])

    w_start(0)
    c_start()

    table = jnp.concatenate([taps[0], taps[1], taps[2], skip[...], jnp.zeros((6, 512), F32)], axis=0)
    coef[...] = table.T

    def build(g8, carry):
        rows8 = filt[pl.ds(pl.multiple_of(g8 * 16, 16), 16), :].astype(F32)
        for r in range(16):
            row = jnp.concatenate([rows8[r:r + 1, :], jnp.zeros((1, 128), F32)], axis=1)
            wide = jnp.broadcast_to(row, (128, 256))
            toep[g8 * 16 + r] = pltpu.roll(wide, 0, 1, stride=1, stride_axis=0).astype(BF)
        return carry

    lax.fori_loop(0, 2, build, 0)

    arrived(tail_in, r_tail)
    tail_cols[...] = jnp.where(ctx == 0, 0.0, tail_in[...]).T

    lane = lax.broadcasted_iota(jnp.int32, (64, 128), 1)

    def featurize(i, carry):
        rows = pl.ds(pl.multiple_of(i * 64, 64), 64)
        co = coef[rows, :]
        tl = tail_cols[rows, :]
        feats = []
        for a in range(3):
            v = inp[a, rows, :].astype(F32)
            t126, t127 = tl[:, 2 * a:2 * a + 1], tl[:, 2 * a + 1:2 * a + 2]
            v1 = jnp.where(lane == 0, t127, pltpu.roll(v, 1, 1))
            v2 = jnp.where(lane == 0, t126, jnp.where(lane == 1, t127, pltpu.roll(v, 2, 1)))
            feats.append(co[:, 3 * a:3 * a + 1] * v + co[:, 3 * a + 1:3 * a + 2] * v1 + co[:, 3 * a + 2:3 * a + 3] * v2)
        qf[rows, :] = feats[0]
        kf[rows, :] = feats[1]
        vf[rows, :] = feats[2]
        prod[rows, :] = (feats[1] * feats[2]).astype(BF)
        return carry

    lax.fori_loop(0, 8, featurize, 0)
    r_prod = new_recv()
    send(prod, prev, r_prod, later)

    w_start(1)
    w_near(0)

    arrived(prev, r_prod)

    @pl.when(ctx == 0)
    def _():
        prev[...] = jnp.zeros((512, 128), BF)

    def convolve(i, carry):
        pieces = []
        for j in range(8):
            rows = pl.ds(pl.multiple_of(i * 128 + j * 16, 16), 16)
            g = i * 8 + j
            cur = prod[rows, :]
            r = nn_dot(cur, toep[g, :, 0:128]) + nn_dot(prev[rows, :], toep[g, :, 128:256])
            r = r + coef[rows, 9:10] * cur.astype(F32)
            resp[rows, :] = r
            pieces.append(qf[rows, :] * r)
        gated_t[:, pl.ds(pl.multiple_of(i * 128, 128), 128)] = jnp.concatenate(pieces, axis=0).T.astype(BF)
        return carry

    lax.fori_loop(0, 2, convolve, 0)
    w_start(2)
    w_far(0)
    c_ynear(0)
    lax.fori_loop(2, 4, convolve, 0)
    w_near(1)
    c_znear()

    acc[...] = jnp.zeros((512, 128), F32)

    def forward(s):
        def one(i, carry):
            n = plus(x, i) * 4 + line[s]
            for k in range(2):
                part[n, :, 256 * k:256 * (k + 1)] = nn_dot(gated_t[...], wall[n, k]).astype(BF)
            return carry

        lax.fori_loop(0, 4, one, 0)

    def backward(s):
        def one(r, carry):
            rows = pl.ds(pl.multiple_of(r * 128, 128), 128)
            total = acc[rows, :]
            for d in range(4):
                n = plus(x, d) * 4 + line[s]
                for k in range(2):
                    total = total + nn_dot(wall[n, k, rows, :], call[n, 256 * k:256 * (k + 1), :])
            acc[rows, :] = total
            return carry

        lax.fori_loop(0, 4, one, 0)

    w_sibling(0)
    forward(0)
    w_start(3)
    w_far(1)
    c_zfar()
    c_yfar(0)
    c_ynear(3)
    c_ynear(1)
    w_near(2)
    w_sibling(1)
    forward(1)
    c_ynear(2)
    c_yfar(3)
    c_yfar(1)
    w_far(2)
    c_yfar(2)
    w_sibling(2)
    forward(2)
    backward(0)
    w_near(3)
    backward(1)
    backward(2)
    w_far(3)
    w_sibling(3)
    forward(3)

    yh = [[new_recv() for _ in range(2)] for _ in range(4)]
    yf = [[new_recv() for _ in range(2)] for _ in range(4)]
    order = [2, 1, 3, 0]
    top, low = pl.ds(0, 64), pl.ds(64, 64)
    for d in order:
        far = plus(zh, d) * 4 + plus(y, 2)
        send(part.at[far, top, :], y_half.at[d, 0], yh[d][0], y_right)
        send(part.at[far, low, :], y_half.at[d, 1], yh[d][1], y_left)
    backward(3)

    def at_response(i, carry):
        rows = pl.ds(pl.multiple_of(i * 64, 64), 64)
        gg = acc[rows, :].astype(BF).astype(F32)
        gout[rows, :] = (gg * qf[rows, :]).astype(BF)
        qf[rows, :] = gg * resp[rows, :]
        return carry

    lax.fori_loop(0, 8, at_response, 0)
    r_gout = new_recv()
    send(gout, gnext, r_gout, earlier)

    for d in order:
        group = plus(zh, d) * 4
        arrived(y_half.at[d, 0], yh[d][0])
        n = group + plus(y, 1)
        y_stage[d, 0, 0:64, :] = (part[n, 0:64, :].astype(F32) + y_half[d, 0].astype(F32)).astype(BF)
        y_stage[d, 0, 64:128, :] = part[n, 64:128, :]
        send(y_stage.at[d, 0], y_full.at[d, 0], yf[d][0], y_right)
        arrived(y_half.at[d, 1], yh[d][1])
        n = group + plus(y, 3)
        y_stage[d, 1, 0:64, :] = part[n, 0:64, :]
        y_stage[d, 1, 64:128, :] = (part[n, 64:128, :].astype(F32) + y_half[d, 1].astype(F32)).astype(BF)
        send(y_stage.at[d, 1], y_full.at[d, 1], yf[d][1], y_left)

    arrived(gnext, r_gout)

    @pl.when(ctx == 31)
    def _():
        gnext[...] = jnp.zeros((512, 128), BF)

    def y_sum(d):
        arrived(y_full.at[d, 0], yf[d][0])
        arrived(y_full.at[d, 1], yf[d][1])
        mine = part[plus(zh, d) * 4 + y].astype(F32)
        return mine + y_full[d, 0].astype(F32) + y_full[d, 1].astype(F32)

    zhs = [new_recv() for _ in range(2)]
    zfs = [new_recv() for _ in range(2)]

    def grad_product(i, carry):
        for j in range(8):
            rows = pl.ds(pl.multiple_of(i * 128 + j * 16, 16), 16)
            g = i * 8 + j
            gr = gout[rows, :]
            r = nt_dot(gr, toep[g, :, 0:128]) + nt_dot(gnext[rows, :], toep[g, :, 128:256])
            r = r + coef[rows, 9:10] * gr.astype(F32)
            k = kf[rows, :]
            kf[rows, :] = r * vf[rows, :]
            vf[rows, :] = r * k
        return carry

    lax.fori_loop(0, 4, grad_product, 0)
    for a, ref in enumerate((qf, kf, vf)):
        gtail_out[2 * a:2 * a + 2, :] = ref[:, 0:128].T[0:2, :]
    gtail_out[6:8, :] = jnp.zeros((2, 512), F32)
    r_gtail = new_recv()
    send(gtail_out, gtail_in, r_gtail, earlier)

    z_stage[2] = y_sum(2).astype(BF)
    send(z_stage.at[2, top, :], z_half.at[0], zhs[0], h_right)
    send(z_stage.at[2, low, :], z_half.at[1], zhs[1], h_left)

    turn = (
        lax.broadcasted_iota(jnp.int32, (128, 128), 0) + lax.broadcasted_iota(jnp.int32, (128, 128), 1) == 127
    ).astype(F32).astype(BF)

    def correlate(i, carry):
        base = pl.multiple_of(i * 128, 128)
        cur = nn_dot(prod[pl.ds(base, 128), :], turn).astype(BF)
        back = nn_dot(prev[pl.ds(base, 128), :], turn).astype(BF)
        sums = []
        for j in range(8):
            gr = gout[pl.ds(pl.multiple_of(i * 128 + j * 16, 16), 16), :]
            one = tn_dot(cur[16 * j:16 * (j + 1), :], gr)
            two = tn_dot(back[16 * j:16 * (j + 1), :], gr)
            both = pltpu.roll(jnp.concatenate([one, two], axis=1), 129, 1, stride=1, stride_axis=0)
            sums.append(jnp.sum(both[:, 0:128], axis=0, keepdims=True))
        pay[0, pl.ds(pl.multiple_of(i * 8, 8), 8), :] = jnp.concatenate(sums, axis=0)
        return carry

    lax.fori_loop(0, 4, correlate, 0)
    for i in range(4):
        both = gout[128 * i:128 * (i + 1), :].astype(F32) * prod[128 * i:128 * (i + 1), :].astype(F32)
        pay[0, 32 + i:33 + i, :] = jnp.sum(both.T, axis=0, keepdims=True)
    pay[0, 36:40, :] = jnp.zeros((4, 128), F32)

    def exchange(stage, targets):
        sems = [new_recv() for _ in targets]
        for i, who in enumerate(targets):
            send(pay.at[stage], pay_in.at[stage, i], sems[i], who)
        return sems

    def collect(stage, sems):
        total = pay[stage]
        for i, sem in enumerate(sems):
            arrived(pay_in.at[stage, i], sem)
            total = total + pay_in[stage, i]
        return total

    px = exchange(0, [x_right, x_left, x_far])

    for d, way, who in ((1, 0, h_right), (3, 1, h_left)):
        s = y_sum(d)
        arrived(z_half.at[way], zhs[way])
        half = z_half[way].astype(F32)
        if way == 0:
            z_stage[d, 0:64, :] = (s[0:64, :] + half).astype(BF)
            z_stage[d, 64:128, :] = s[64:128, :].astype(BF)
        else:
            z_stage[d, 0:64, :] = s[0:64, :].astype(BF)
            z_stage[d, 64:128, :] = (s[64:128, :] + half).astype(BF)
        send(z_stage.at[d], z_full.at[way], zfs[way], who)

    z_own[...] = y_sum(0)
    pay[1] = collect(0, px)
    pz = exchange(1, [l_up, l_down, l_far])

    arrived(gtail_in, r_gtail)
    gtail_cols[...] = jnp.where(ctx == 31, 0.0, gtail_in[...]).T

    def short_back(i, carry):
        rows = pl.ds(pl.multiple_of(i * 64, 64), 64)
        co = coef[rows, :]
        tl = gtail_cols[rows, :]
        for a, ref in enumerate((qf, kf, vf)):
            v = ref[rows, :]
            t0, t1 = tl[:, 2 * a:2 * a + 1], tl[:, 2 * a + 1:2 * a + 2]
            v1 = jnp.where(lane == 127, t0, pltpu.roll(v, 127, 1))
            v2 = jnp.where(lane == 126, t0, jnp.where(lane == 127, t1, pltpu.roll(v, 126, 1)))
            r = co[:, 3 * a:3 * a + 1] * v + co[:, 3 * a + 1:3 * a + 2] * v1 + co[:, 3 * a + 2:3 * a + 3] * v2
            ginp[a, rows, :] = r.astype(BF)
        return carry

    lax.fori_loop(0, 8, short_back, 0)
    pay[2] = collect(1, pz)
    pc = exchange(2, [sibling])
    total = collect(2, pc)
    gfilt[...] = total[0:32, :]
    gskip[...] = total[32:40, :]

    arrived(z_full.at[0], zfs[0])
    arrived(z_full.at[1], zfs[1])
    final = z_own[...] + z_full[0].astype(F32) + z_full[1].astype(F32)
    out[...] = final.T.astype(BF)

    for copy, when in sends:
        if when is None:
            copy.wait_send()
        else:
            pl.when(when)(lambda copy=copy: copy.wait_send())
    assert count["s"] <= N_SEND and count["r"] <= N_RECV


def body(inputs, short_filters, explicit_filter, skip_gain, out_weight, out_cotangent):
    vmem = pl.BlockSpec(memory_space=pltpu.VMEM)
    hbm = pl.BlockSpec(memory_space=pl.ANY)
    out, ginp, gfilt, gskip = pl.pallas_call(
        kernel,
        out_shape=(
            jax.ShapeDtypeStruct((512, 128), BF),
            jax.ShapeDtypeStruct((3, 512, 128), BF),
            jax.ShapeDtypeStruct((32, 128), F32),
            jax.ShapeDtypeStruct((8, 128), F32),
        ),
        in_specs=[vmem, vmem, vmem, vmem, hbm, hbm],
        out_specs=(vmem, vmem, vmem, vmem),
        scratch_shapes=[
            pltpu.VMEM((16, 2, 512, 256), BF),
            pltpu.VMEM((16, 512, 128), BF),
            pltpu.VMEM((32, 128, 256), BF),
            pltpu.VMEM((512, 16), F32),
            pltpu.VMEM((8, 512), F32),
            pltpu.VMEM((8, 512), F32),
            pltpu.VMEM((512, 8), F32),
            pltpu.VMEM((512, 128), F32),
            pltpu.VMEM((512, 128), F32),
            pltpu.VMEM((512, 128), F32),
            pltpu.VMEM((512, 128), BF),
            pltpu.VMEM((512, 128), BF),
            pltpu.VMEM((512, 128), F32),
            pltpu.VMEM((128, 512), BF),
            pltpu.VMEM((512, 128), F32),
            pltpu.VMEM((16, 128, 512), BF),
            pltpu.VMEM((512, 128), BF),
            pltpu.VMEM((512, 128), BF),
            pltpu.VMEM((8, 128), F32),
            pltpu.VMEM((8, 512), F32),
            pltpu.VMEM((8, 512), F32),
            pltpu.VMEM((512, 8), F32),
            pltpu.VMEM((4, 2, 64, 512), BF),
            pltpu.VMEM((4, 2, 128, 512), BF),
            pltpu.VMEM((4, 2, 128, 512), BF),
            pltpu.VMEM((2, 64, 512), BF),
            pltpu.VMEM((2, 128, 512), BF),
            pltpu.VMEM((4, 128, 512), BF),
            pltpu.VMEM((128, 512), F32),
            pltpu.VMEM((3, 40, 128), F32),
            pltpu.VMEM((3, 3, 40, 128), F32),
            pltpu.SemaphoreType.DMA((2,)),
            pltpu.SemaphoreType.DMA((N_SEND,)),
            pltpu.SemaphoreType.DMA((N_RECV,)),
            pltpu.SemaphoreType.DMA((4,)),
            pltpu.SemaphoreType.DMA((16,)),
        ],
        compiler_params=pltpu.CompilerParams(
            collective_id=0, has_side_effects=True, vmem_limit_bytes=48 * 1024 * 1024
        ),
        cost_estimate=pl.CostEstimate(flops=2600000000, bytes_accessed=4000000, transcendentals=0),
    )(inputs, short_filters, explicit_filter, skip_gain.reshape(1, 512), out_weight, out_cotangent)
    return (out, ginp, gfilt, gskip[0:4].reshape(512))


def solution(mesh):
    placed = (
        P(None, "tp", "ctx"),
        P(None, None, "tp"),
        P("tp", None),
        P("tp"),
        P("tp", "ctx"),
        P("tp", "ctx"),
    )
    return jax.shard_map(
        body,
        mesh=mesh,
        in_specs=placed,
        out_specs=(P("tp", "ctx"), P(None, "tp", "ctx"), P("tp", None), P("tp")),
        check_vma=False,
    )
```

```python
import jax
import jax.numpy as jnp
from jax import lax
from jax.experimental import pallas as pl
from jax.experimental.pallas import tpu as pltpu
from jax.sharding import PartitionSpec as P

MESH = pl.DeviceIdType.MESH
BF = jnp.bfloat16
F32 = jnp.float32
N_SEND = 128
N_RECV = 128


def nt_dot(a, b):
    return lax.dot_general(a, b, (((1,), (1,)), ((), ())), preferred_element_type=F32)


def tn_dot(a, b):
    return lax.dot_general(a, b, (((0,), (0,)), ((), ())), preferred_element_type=F32)


def nn_dot(a, b):
    return jnp.dot(a, b, preferred_element_type=F32)


def kernel(
    inp_hbm, taps_hbm, filt_hbm, skip_hbm, w_hbm, cot_hbm,
    out, ginp, gfilt, gskip,
    inp, taps, filt, skip, wall, call, toep, coef, tail_out, tail_in, tail_cols, qf, kf, vf, prod, prev, resp, gated_t,
    acc, acc_in, part, gout, gnext, gtail_out, gtail_in, gtail_cols,
    y_half, y_full, y_stage, z_half, z_full, z_stage, z_own, fin, fin_out, fin_in,
    pay, pay_in, local_sem, ssem, rsem, wz_sem,
):
    ctx, tp = lax.axis_index("ctx"), lax.axis_index("tp")
    x, zl, core = ctx // 8, (ctx // 2) % 4, ctx % 2
    zh, y = tp // 4, tp % 4
    own = x * 4 + zl

    local = [
        pltpu.make_async_copy(w_hbm, wall.at[own], local_sem.at[0]),
        pltpu.make_async_copy(inp_hbm, inp, local_sem.at[1]),
        pltpu.make_async_copy(taps_hbm, taps, local_sem.at[2]),
        pltpu.make_async_copy(skip_hbm, skip, local_sem.at[3]),
        pltpu.make_async_copy(filt_hbm, filt, local_sem.at[4]),
        pltpu.make_async_copy(cot_hbm.at[pl.ds(pl.multiple_of(core * 256, 256), 256), :], call.at[tp, core], local_sem.at[5]),
    ]
    for copy in local:
        copy.start()

    def at_ctx(x_, zl_, core_):
        return ((x_ * 4 + zl_) * 2 + core_, tp)

    def at_tp(zh_, y_):
        return (ctx, zh_ * 4 + y_)

    def plus(v, d):
        return (v + d) % 4

    x_right, x_left, x_far = at_ctx(plus(x, 1), zl, core), at_ctx(plus(x, 3), zl, core), at_ctx(plus(x, 2), zl, core)
    l_up, l_down, l_far = at_ctx(x, plus(zl, 1), core), at_ctx(x, plus(zl, 3), core), at_ctx(x, plus(zl, 2), core)
    sibling = at_ctx(x, zl, 1 - core)
    later, earlier = ((ctx + 1) % 32, tp), ((ctx + 31) % 32, tp)
    h_right, h_left = at_tp(plus(zh, 1), y), at_tp(plus(zh, 3), y)
    y_right, y_left = at_tp(zh, plus(y, 1)), at_tp(zh, plus(y, 3))

    upper = zl // 2
    inner = zl + upper * (3 - 2 * zl)
    step_dir = 1 - 2 * upper
    z_in = at_ctx(x, zl + step_dir, core)
    z_out = at_ctx(x, (zl - step_dir + 4) % 4, core)

    def unmirror(v):
        return v + upper * (3 - 2 * v)

    line = [zl, unmirror(1 - inner), unmirror(2), unmirror(3)]

    partners = [x_right, x_left, x_far, l_up, l_down, l_far, sibling, later, earlier, h_right, h_left, y_right, y_left]
    barrier = pltpu.get_barrier_semaphore()
    for who in partners:
        pl.semaphore_signal(barrier, inc=1, device_id=who, device_id_type=MESH)

    count = {"s": 0, "r": 0}
    sends = []

    def new_recv():
        count["r"] += 1
        return rsem.at[count["r"] - 1]

    def new_send():
        count["s"] += 1
        return ssem.at[count["s"] - 1]

    def send(src, dst, sem, who, when=None):
        copy = pltpu.make_async_remote_copy(src, dst, new_send(), sem, device_id=who, device_id_type=MESH)
        if when is None:
            copy.start()
        else:
            pl.when(when)(lambda: copy.start())
        sends.append((copy, when))

    def arrived(dst, sem):
        pltpu.make_async_remote_copy(dst, dst, ssem.at[0], sem, device_id=sibling, device_id_type=MESH).wait_recv()

    local[1].wait()
    for a in range(3):
        turned = inp[a].astype(F32).T
        tail_out[2 * a:2 * a + 2, :] = turned[126:128, :]
    tail_out[6:8, :] = jnp.zeros((2, 512), F32)
    for copy in (local[2], local[3], local[4], local[5], local[0]):
        copy.wait()
    pl.semaphore_wait(barrier, len(partners))

    x_sems = [[new_recv() for _ in range(4)] for _ in range(4)]
    lo, hi = pl.ds(0, 256), pl.ds(256, 256)

    def w_start(s):
        n = x * 4 + line[s]
        block = wall.at[n]
        if s > 0:
            arrived(block, wz_sem.at[line[s]])
        if s == 0:
            send(block, block, wz_sem.at[line[s]], z_in)
            send(block, block, wz_sem.at[line[s]], z_out, inner == 1)
        elif s == 1:
            send(block, block, wz_sem.at[line[s]], z_in, inner == 1)
        else:
            send(block, block, wz_sem.at[line[s]], z_out, inner == 1)
        send(block, block, x_sems[s][0], x_right)
        send(block, block, x_sems[s][1], x_left)

    def w_near(s):
        n = plus(x, 3) * 4 + line[s]
        arrived(wall.at[n], x_sems[s][0])
        half = wall.at[n, lo, :]
        send(half, half, x_sems[s][2], x_right)
        n = plus(x, 1) * 4 + line[s]
        arrived(wall.at[n], x_sems[s][1])
        half = wall.at[n, hi, :]
        send(half, half, x_sems[s][3], x_left)

    def w_far(s):
        n = plus(x, 2) * 4 + line[s]
        arrived(wall.at[n, lo, :], x_sems[s][2])
        arrived(wall.at[n, hi, :], x_sems[s][3])

    r_cot = new_recv()
    c_zn = [[new_recv() for _ in range(2)] for _ in range(2)]
    c_zf = [new_recv() for _ in range(2)]
    c_ys = [[new_recv() for _ in range(4)] for _ in range(4)]

    def c_zsend(p):
        block = call.at[tp, p]
        send(block, block, c_zn[p][0], h_right)
        send(block, block, c_zn[p][1], h_left)

    def c_zforward(p):
        n = plus(zh, 3 - 2 * p) * 4 + y
        block = call.at[n, p]
        arrived(block, c_zn[p][p])
        send(block, block, c_zf[p], (h_right, h_left)[p])

    def c_znear(d):
        n = plus(zh, d) * 4 + y
        way = (3 - d) // 2
        arrived(call.at[n, 1 - way], c_zn[1 - way][way])

    def c_zfar():
        n = plus(zh, 2) * 4 + y
        arrived(call.at[n, 0], c_zf[0])
        arrived(call.at[n, 1], c_zf[1])

    def c_ysend(d):
        block = call.at[plus(zh, d) * 4 + y]
        send(block, block, c_ys[d][0], y_right)
        send(block, block, c_ys[d][1], y_left)

    def c_ynear(d):
        n = plus(zh, d) * 4 + plus(y, 3)
        arrived(call.at[n], c_ys[d][0])
        send(call.at[n, 0], call.at[n, 0], c_ys[d][2], y_right)
        n = plus(zh, d) * 4 + plus(y, 1)
        arrived(call.at[n], c_ys[d][1])
        send(call.at[n, 1], call.at[n, 1], c_ys[d][3], y_left)

    def c_yfar(d):
        n = plus(zh, d) * 4 + plus(y, 2)
        arrived(call.at[n, 0], c_ys[d][2])
        arrived(call.at[n, 1], c_ys[d][3])

    def build(g16, carry):
        rows16 = filt[pl.ds(pl.multiple_of(g16 * 16, 16), 16), :].astype(F32)
        for r in range(16):
            row = jnp.concatenate([rows16[r:r + 1, :], jnp.zeros((1, 128), F32)], axis=1)
            wide = jnp.broadcast_to(row, (128, 256))
            toep[g16 * 16 + r] = pltpu.roll(wide, 0, 1, stride=1, stride_axis=0).astype(BF)
        return carry

    lane = lax.broadcasted_iota(jnp.int32, (64, 128), 1)

    def featurize(i, carry):
        rows = pl.ds(pl.multiple_of(i * 64, 64), 64)
        co = coef[rows, :]
        tl = tail_cols[rows, :]
        feats = []
        for a in range(3):
            v = inp[a, rows, :].astype(F32)
            t126, t127 = tl[:, 2 * a:2 * a + 1], tl[:, 2 * a + 1:2 * a + 2]
            v1 = jnp.where(lane == 0, t127, pltpu.roll(v, 1, 1))
            v2 = jnp.where(lane == 0, t126, jnp.where(lane == 1, t127, pltpu.roll(v, 2, 1)))
            feats.append(co[:, 3 * a:3 * a + 1] * v + co[:, 3 * a + 1:3 * a + 2] * v1 + co[:, 3 * a + 2:3 * a + 3] * v2)
        qf[rows, :] = feats[0]
        kf[rows, :] = feats[1]
        vf[rows, :] = feats[2]
        prod[rows, :] = (feats[1] * feats[2]).astype(BF)
        return carry

    def convolve(i, carry):
        pieces = []
        for j in range(8):
            rows = pl.ds(pl.multiple_of(i * 128 + j * 16, 16), 16)
            g = i * 8 + j
            cur = prod[rows, :]
            r = nn_dot(cur, toep[g, :, 0:128]) + nn_dot(prev[rows, :], toep[g, :, 128:256])
            r = r + coef[rows, 9:10] * cur.astype(F32)
            resp[rows, :] = r
            pieces.append(qf[rows, :] * r)
        columns = pl.ds(pl.multiple_of(i * 128, 128), 128)
        gated_t[core, :, columns] = jnp.concatenate(pieces, axis=0).T.astype(BF)
        return carry

    def forward(dx, steps):
        tokens = jnp.concatenate([gated_t[0], gated_t[1]], axis=0)
        for s in steps:
            n = plus(x, dx) * 4 + line[s]
            r = nn_dot(tokens, wall[n]).astype(BF)
            part[n, 0] = r[0:128, :]
            part[n, 1] = r[128:256, :]

    def backward(dx, steps, first=False):
        def one(r, carry):
            rows = pl.ds(pl.multiple_of(r * 128, 128), 128)
            total = None if first else jnp.concatenate([acc[0, rows, :], acc[1, rows, :]], axis=1)
            for s in steps:
                n = plus(x, dx) * 4 + line[s]
                term = nn_dot(wall[n, rows, :], jnp.concatenate([call[n, 0], call[n, 1]], axis=1))
                total = term if total is None else total + term
            acc[0, rows, :] = total[:, 0:128]
            acc[1, rows, :] = total[:, 128:256]
            return carry

        lax.fori_loop(0, 4, one, 0)

    yh = [[new_recv() for _ in range(2)] for _ in range(4)]
    yf = [[new_recv() for _ in range(2)] for _ in range(4)]
    zhs = [new_recv() for _ in range(2)]
    zfs = [new_recv() for _ in range(2)]
    zss = [new_send() for _ in range(4)]

    def y_begin(dx):
        far = plus(zh, dx) * 4 + plus(y, 2)
        send(part.at[far, 0], y_half.at[dx, 0], yh[dx][0], y_right)
        send(part.at[far, 1], y_half.at[dx, 1], yh[dx][1], y_left)

    def y_merge(dx):
        group = plus(zh, dx) * 4
        for way, who in ((0, y_right), (1, y_left)):
            n = group + plus(y, 1 + 2 * way)
            arrived(y_half.at[dx, way], yh[dx][way])
            y_stage[dx, way, way] = (part[n, way].astype(F32) + y_half[dx, way].astype(F32)).astype(BF)
            y_stage[dx, way, 1 - way] = part[n, 1 - way]
            send(y_stage.at[dx, way], y_full.at[dx, way], yf[dx][way], who)

    z_far = [
        pltpu.make_async_remote_copy(z_stage.at[0, i], z_half.at[i], zss[i], zhs[i], device_id=who, device_id_type=MESH)
        for i, who in enumerate((h_right, h_left))
    ]
    z_near = [
        pltpu.make_async_remote_copy(z_stage.at[1 + i], z_full.at[i], zss[2 + i], zfs[i], device_id=who, device_id_type=MESH)
        for i, who in enumerate((h_right, h_left))
    ]

    def y_sum(d):
        arrived(y_full.at[d, 0], yf[d][0])
        arrived(y_full.at[d, 1], yf[d][1])
        n = plus(zh, d) * 4 + y
        return [
            part[n, i].astype(F32) + y_full[d, 0, i].astype(F32) + y_full[d, 1, i].astype(F32) for i in range(2)
        ]

    def z_first():
        sums = y_sum(2)
        for i in range(2):
            z_stage[0, i] = sums[i].astype(BF)
            z_far[i].start()

    def z_second(way):
        sums = y_sum(1 + 2 * way)
        z_stage[1 + way, 1 - way] = sums[1 - way].astype(BF)
        arrived(z_half.at[way], zhs[way])
        z_stage[1 + way, way] = (sums[way] + z_half[way].astype(F32)).astype(BF)
        z_near[way].start()

    def z_third():
        sums = y_sum(0)
        for i in range(2):
            z_own[i] = sums[i]

    turn = (
        lax.broadcasted_iota(jnp.int32, (128, 128), 0) + lax.broadcasted_iota(jnp.int32, (128, 128), 1) == 127
    ).astype(F32).astype(BF)

    def at_response(i, carry):
        rows = pl.ds(pl.multiple_of(i * 64, 64), 64)
        gg = (acc[core, rows, :] + acc_in[rows, :]).astype(BF).astype(F32)
        gout[rows, :] = (gg * qf[rows, :]).astype(BF)
        qf[rows, :] = gg * resp[rows, :]
        return carry

    def grad_product(i, carry):
        for j in range(8):
            rows = pl.ds(pl.multiple_of(i * 128 + j * 16, 16), 16)
            g = i * 8 + j
            gr = gout[rows, :]
            r = nt_dot(gr, toep[g, :, 0:128]) + nt_dot(gnext[rows, :], toep[g, :, 128:256])
            r = r + coef[rows, 9:10] * gr.astype(F32)
            k = kf[rows, :]
            kf[rows, :] = r * vf[rows, :]
            vf[rows, :] = r * k
        return carry

    def correlate(i, carry):
        base = pl.multiple_of(i * 128, 128)
        cur = nn_dot(prod[pl.ds(base, 128), :], turn).astype(BF)
        back = nn_dot(prev[pl.ds(base, 128), :], turn).astype(BF)
        sums = []
        for j in range(8):
            gr = gout[pl.ds(pl.multiple_of(i * 128 + j * 16, 16), 16), :]
            one = tn_dot(cur[16 * j:16 * (j + 1), :], gr)
            two = tn_dot(back[16 * j:16 * (j + 1), :], gr)
            both = pltpu.roll(jnp.concatenate([one, two], axis=1), 129, 1, stride=1, stride_axis=0)
            sums.append(jnp.sum(both[:, 0:128], axis=0, keepdims=True))
        pay[0, pl.ds(pl.multiple_of(i * 8, 8), 8), :] = jnp.concatenate(sums, axis=0)
        return carry

    def exchange(stage, targets):
        sems = [new_recv() for _ in targets]
        for i, who in enumerate(targets):
            send(pay.at[stage], pay_in.at[stage, i], sems[i], who)
        return sems

    def collect(stage, sems):
        total = pay[stage]
        for i, sem in enumerate(sems):
            arrived(pay_in.at[stage, i], sem)
            total = total + pay_in[stage, i]
        return total

    def short_back(i, carry):
        rows = pl.ds(pl.multiple_of(i * 64, 64), 64)
        co = coef[rows, :]
        tl = gtail_cols[rows, :]
        for a, ref in enumerate((qf, kf, vf)):
            v = ref[rows, :]
            t0, t1 = tl[:, 2 * a:2 * a + 1], tl[:, 2 * a + 1:2 * a + 2]
            v1 = jnp.where(lane == 127, t0, pltpu.roll(v, 127, 1))
            v2 = jnp.where(lane == 126, t0, jnp.where(lane == 127, t1, pltpu.roll(v, 126, 1)))
            r = co[:, 3 * a:3 * a + 1] * v + co[:, 3 * a + 1:3 * a + 2] * v1 + co[:, 3 * a + 2:3 * a + 3] * v2
            ginp[a, rows, :] = r.astype(BF)
        return carry

    w_start(0)
    r_tail = new_recv()
    send(tail_out, tail_in, r_tail, later)
    theirs = pl.ds(pl.multiple_of((1 - core) * 256, 256), 256)
    send(cot_hbm.at[theirs, :], call.at[tp, core], r_cot, sibling)

    table = jnp.concatenate([taps[0], taps[1], taps[2], skip[...], jnp.zeros((6, 512), F32)], axis=0)
    coef[...] = table.T
    arrived(tail_in, r_tail)
    tail_cols[...] = jnp.where(ctx == 0, 0.0, tail_in[...]).T
    lax.fori_loop(0, 8, featurize, 0)
    r_prod = new_recv()
    send(prod, prev, r_prod, later)
    arrived(call.at[tp, 1 - core], r_cot)
    c_zsend(0)
    c_zsend(1)
    c_ysend(0)
    lax.fori_loop(0, 2, build, 0)

    w_start(1)
    w_near(0)
    arrived(prev, r_prod)

    @pl.when(ctx == 0)
    def _():
        prev[...] = jnp.zeros((512, 128), BF)

    lax.fori_loop(0, 4, convolve, 0)
    r_gated = new_recv()
    send(gated_t.at[core], gated_t.at[core], r_gated, sibling)
    w_start(2)
    c_ynear(0)
    w_near(1)
    c_zforward(0)
    c_zforward(1)
    c_znear(3)
    c_znear(1)
    c_ysend(3)
    c_ysend(1)
    arrived(gated_t.at[1 - core], r_gated)
    w_start(3)
    w_far(0)
    forward(0, (0, 1, 2, 3))
    for d in (3, 1, 2):
        forward(d, (0,))
    c_zfar()
    c_ysend(2)
    w_near(2)
    c_yfar(0)
    c_ynear(3)
    c_ynear(1)
    w_far(1)
    for d in (3, 1, 2):
        forward(d, (1,))
    w_near(3)
    c_ynear(2)
    c_yfar(3)
    c_yfar(1)
    c_yfar(2)
    w_far(2)
    forward(3, (2, 3))
    forward(1, (2, 3))
    forward(2, (2,))
    backward(0, (0, 1, 2, 3), True)
    backward(3, (0, 1, 2, 3))
    backward(1, (0, 1, 2, 3))
    w_far(3)
    forward(2, (3,))
    for d in (2, 1, 3, 0):
        y_begin(d)
    backward(2, (0, 1, 2, 3))
    r_acc = new_recv()
    send(acc.at[1 - core], acc_in, r_acc, sibling)
    arrived(acc_in, r_acc)
    lax.fori_loop(0, 8, at_response, 0)
    r_gout = new_recv()
    send(gout, gnext, r_gout, earlier)
    for d in (2, 1, 3, 0):
        y_merge(d)
    arrived(gnext, r_gout)

    @pl.when(ctx == 31)
    def _():
        gnext[...] = jnp.zeros((512, 128), BF)

    lax.fori_loop(0, 4, grad_product, 0)
    for a, ref in enumerate((qf, kf, vf)):
        gtail_out[2 * a:2 * a + 2, :] = ref[:, 0:128].T[0:2, :]
    gtail_out[6:8, :] = jnp.zeros((2, 512), F32)
    r_gtail = new_recv()
    send(gtail_out, gtail_in, r_gtail, earlier)
    z_first()
    lax.fori_loop(0, 4, correlate, 0)
    for i in range(4):
        both = gout[128 * i:128 * (i + 1), :].astype(F32) * prod[128 * i:128 * (i + 1), :].astype(F32)
        pay[0, 32 + i:33 + i, :] = jnp.sum(both.T, axis=0, keepdims=True)
    pay[0, 36:40, :] = jnp.zeros((4, 128), F32)
    px = exchange(0, [x_right, x_left, x_far])
    z_second(0)
    z_second(1)
    z_third()
    pay[1] = collect(0, px)
    pz = exchange(1, [l_up, l_down, l_far])

    arrived(gtail_in, r_gtail)
    gtail_cols[...] = jnp.where(ctx == 31, 0.0, gtail_in[...]).T
    lax.fori_loop(0, 8, short_back, 0)
    pay[2] = collect(1, pz)
    pc = exchange(2, [sibling])

    arrived(z_full.at[0], zfs[0])
    arrived(z_full.at[1], zfs[1])
    fin[...] = z_own[...] + z_full[0].astype(F32) + z_full[1].astype(F32)
    fin_out[...] = fin[1 - core].astype(BF)
    r_fin = new_recv()
    send(fin_out, fin_in, r_fin, sibling)
    out[pl.ds(pl.multiple_of(core * 256, 256), 256), :] = fin[core].T.astype(BF)
    total = collect(2, pc)
    gfilt[...] = total[0:32, :]
    gskip[...] = total[32:40, :]
    arrived(fin_in, r_fin)
    out[theirs, :] = fin_in[...].astype(F32).T.astype(BF)

    for copy, when in sends:
        if when is None:
            copy.wait_send()
        else:
            pl.when(when)(lambda copy=copy: copy.wait_send())
    for copy in z_far + z_near:
        copy.wait_send()
    assert count["s"] <= N_SEND and count["r"] <= N_RECV


def body(inputs, short_filters, explicit_filter, skip_gain, out_weight, out_cotangent):
    vmem = pl.BlockSpec(memory_space=pltpu.VMEM)
    hbm = pl.BlockSpec(memory_space=pltpu.HBM)
    out, ginp, gfilt, gskip = pl.pallas_call(
        kernel,
        out_shape=(
            jax.ShapeDtypeStruct((512, 128), BF),
            jax.ShapeDtypeStruct((3, 512, 128), BF),
            jax.ShapeDtypeStruct((32, 128), F32),
            jax.ShapeDtypeStruct((8, 128), F32),
        ),
        in_specs=[hbm] * 6,
        out_specs=(vmem, vmem, vmem, vmem),
        scratch_shapes=[
            pltpu.VMEM((3, 512, 128), BF),
            pltpu.VMEM((3, 3, 512), F32),
            pltpu.VMEM((32, 128), BF),
            pltpu.VMEM((1, 512), F32),
            pltpu.VMEM((16, 512, 256), BF),
            pltpu.VMEM((16, 2, 256, 128), BF),
            pltpu.VMEM((32, 128, 256), BF),
            pltpu.VMEM((512, 16), F32),
            pltpu.VMEM((8, 512), F32),
            pltpu.VMEM((8, 512), F32),
            pltpu.VMEM((512, 8), F32),
            pltpu.VMEM((512, 128), F32),
            pltpu.VMEM((512, 128), F32),
            pltpu.VMEM((512, 128), F32),
            pltpu.VMEM((512, 128), BF),
            pltpu.VMEM((512, 128), BF),
            pltpu.VMEM((512, 128), F32),
            pltpu.VMEM((2, 128, 512), BF),
            pltpu.VMEM((2, 512, 128), F32),
            pltpu.VMEM((512, 128), F32),
            pltpu.VMEM((16, 2, 128, 256), BF),
            pltpu.VMEM((512, 128), BF),
            pltpu.VMEM((512, 128), BF),
            pltpu.VMEM((8, 512), F32),
            pltpu.VMEM((8, 512), F32),
            pltpu.VMEM((512, 8), F32),
            pltpu.VMEM((4, 2, 128, 256), BF),
            pltpu.VMEM((4, 2, 2, 128, 256), BF),
            pltpu.VMEM((4, 2, 2, 128, 256), BF),
            pltpu.VMEM((2, 128, 256), BF),
            pltpu.VMEM((2, 2, 128, 256), BF),
            pltpu.VMEM((3, 2, 128, 256), BF),
            pltpu.VMEM((2, 128, 256), F32),
            pltpu.VMEM((2, 128, 256), F32),
            pltpu.VMEM((128, 256), BF),
            pltpu.VMEM((128, 256), BF),
            pltpu.VMEM((3, 40, 128), F32),
            pltpu.VMEM((3, 3, 40, 128), F32),
            pltpu.SemaphoreType.DMA((6,)),
            pltpu.SemaphoreType.DMA((N_SEND,)),
            pltpu.SemaphoreType.DMA((N_RECV,)),
            pltpu.SemaphoreType.DMA((4,)),
        ],
        compiler_params=pltpu.CompilerParams(
            collective_id=0, has_side_effects=True, vmem_limit_bytes=60 * 1024 * 1024
        ),
        cost_estimate=pl.CostEstimate(flops=2600000000, bytes_accessed=4000000, transcendentals=0),
    )(inputs, short_filters, explicit_filter, skip_gain.reshape(1, 512), out_weight, out_cotangent)
    return (out, ginp, gfilt, gskip[0:4].reshape(512))


def solution(mesh):
    placed = (
        P(None, "tp", "ctx"),
        P(None, None, "tp"),
        P("tp", None),
        P("tp"),
        P("tp", "ctx"),
        P("tp", "ctx"),
    )
    return jax.shard_map(
        body,
        mesh=mesh,
        in_specs=placed,
        out_specs=(P("tp", "ctx"), P(None, "tp", "ctx"), P("tp", None), P("tp")),
        check_vma=False,
    )
```

```python
import jax
import jax.numpy as jnp
from jax import lax
from jax.experimental import pallas as pl
from jax.experimental.pallas import tpu as pltpu
from jax.sharding import PartitionSpec as P

MESH = pl.DeviceIdType.MESH
BF = jnp.bfloat16
F32 = jnp.float32
N_SEND = 128
N_RECV = 128


def nt_dot(a, b):
    return lax.dot_general(a, b, (((1,), (1,)), ((), ())), preferred_element_type=F32)


def tn_dot(a, b):
    return lax.dot_general(a, b, (((0,), (0,)), ((), ())), preferred_element_type=F32)


def nn_dot(a, b):
    return jnp.dot(a, b, preferred_element_type=F32)


def kernel(
    inp_hbm, taps_hbm, filt_hbm, skip_hbm, w_hbm, cot_hbm,
    out, ginp, gfilt, gskip,
    inp, taps, filt, skip, wall, call, toep, coef, tail_out, tail_in, tail_cols, qf, kf, vf, prod, prev, resp, gated_t,
    acc, acc_in, part, gout, gnext, gtail_out, gtail_in, gtail_cols,
    y_half, y_full, y_stage, z_half, z_full, z_stage, z_own, z_mid, fin, fin_out, fin_in,
    pay, pay_in, local_sem, ssem, rsem, wz_sem, y_sem,
):
    ctx, tp = lax.axis_index("ctx"), lax.axis_index("tp")
    x, zl, core = ctx // 8, (ctx // 2) % 4, ctx % 2
    zh, y = tp // 4, tp % 4
    own = x * 4 + zl

    local = [
        pltpu.make_async_copy(w_hbm, wall.at[own], local_sem.at[0]),
        pltpu.make_async_copy(inp_hbm, inp, local_sem.at[1]),
        pltpu.make_async_copy(taps_hbm, taps, local_sem.at[2]),
        pltpu.make_async_copy(skip_hbm, skip, local_sem.at[3]),
        pltpu.make_async_copy(filt_hbm, filt, local_sem.at[4]),
        pltpu.make_async_copy(cot_hbm.at[pl.ds(pl.multiple_of(core * 256, 256), 256), :], call.at[tp, core], local_sem.at[5]),
    ]
    for copy in local:
        copy.start()

    def at_ctx(x_, zl_, core_):
        return ((x_ * 4 + zl_) * 2 + core_, tp)

    def at_tp(zh_, y_):
        return (ctx, zh_ * 4 + y_)

    def plus(v, d):
        return (v + d) % 4

    x_right, x_left, x_far = at_ctx(plus(x, 1), zl, core), at_ctx(plus(x, 3), zl, core), at_ctx(plus(x, 2), zl, core)
    l_up, l_down, l_far = at_ctx(x, plus(zl, 1), core), at_ctx(x, plus(zl, 3), core), at_ctx(x, plus(zl, 2), core)
    sibling = at_ctx(x, zl, 1 - core)
    later, earlier = ((ctx + 1) % 32, tp), ((ctx + 31) % 32, tp)
    h_right, h_left = at_tp(plus(zh, 1), y), at_tp(plus(zh, 3), y)
    y_right, y_left = at_tp(zh, plus(y, 1)), at_tp(zh, plus(y, 3))

    upper = zl // 2
    inner = zl + upper * (3 - 2 * zl)
    step_dir = 1 - 2 * upper
    z_in = at_ctx(x, zl + step_dir, core)
    z_out = at_ctx(x, (zl - step_dir + 4) % 4, core)

    def unmirror(v):
        return v + upper * (3 - 2 * v)

    line = [zl, unmirror(1 - inner), unmirror(2), unmirror(3)]

    partners = [x_right, x_left, x_far, l_up, l_down, l_far, sibling, later, earlier, h_right, h_left, y_right, y_left]
    barrier = pltpu.get_barrier_semaphore()
    for who in partners:
        pl.semaphore_signal(barrier, inc=1, device_id=who, device_id_type=MESH)

    count = {"s": 0, "r": 0}
    sends = []

    def new_recv():
        count["r"] += 1
        return rsem.at[count["r"] - 1]

    def new_send():
        count["s"] += 1
        return ssem.at[count["s"] - 1]

    def send(src, dst, sem, who, when=None):
        copy = pltpu.make_async_remote_copy(src, dst, new_send(), sem, device_id=who, device_id_type=MESH)
        if when is None:
            copy.start()
        else:
            pl.when(when)(lambda: copy.start())
        sends.append((copy, when))

    def arrived(dst, sem):
        pltpu.make_async_remote_copy(dst, dst, ssem.at[0], sem, device_id=sibling, device_id_type=MESH).wait_recv()

    local[1].wait()
    for a in range(3):
        turned = inp[a].astype(F32).T
        tail_out[2 * a:2 * a + 2, :] = turned[126:128, :]
    tail_out[6:8, :] = jnp.zeros((2, 512), F32)
    for copy in (local[2], local[3], local[4], local[5], local[0]):
        copy.wait()
    pl.semaphore_wait(barrier, len(partners))

    x_sems = [[new_recv() for _ in range(4)] for _ in range(4)]
    lo, hi = pl.ds(0, 256), pl.ds(256, 256)

    def w_start(s):
        n = x * 4 + line[s]
        block = wall.at[n]
        if s > 0:
            arrived(block, wz_sem.at[line[s]])
        if s == 0:
            send(block, block, wz_sem.at[line[s]], z_in)
            send(block, block, wz_sem.at[line[s]], z_out, inner == 1)
        elif s == 1:
            send(block, block, wz_sem.at[line[s]], z_in, inner == 1)
        else:
            send(block, block, wz_sem.at[line[s]], z_out, inner == 1)
        send(block, block, x_sems[s][0], x_right)
        send(block, block, x_sems[s][1], x_left)

    def w_near(s):
        n = plus(x, 3) * 4 + line[s]
        arrived(wall.at[n], x_sems[s][0])
        half = wall.at[n, lo, :]
        send(half, half, x_sems[s][2], x_right)
        n = plus(x, 1) * 4 + line[s]
        arrived(wall.at[n], x_sems[s][1])
        half = wall.at[n, hi, :]
        send(half, half, x_sems[s][3], x_left)

    def w_far(s):
        n = plus(x, 2) * 4 + line[s]
        arrived(wall.at[n, lo, :], x_sems[s][2])
        arrived(wall.at[n, hi, :], x_sems[s][3])

    r_cot = new_recv()
    c_zn = [[new_recv() for _ in range(2)] for _ in range(2)]
    c_zf = [new_recv() for _ in range(2)]
    c_ys = [[new_recv() for _ in range(4)] for _ in range(4)]

    def c_zsend(p):
        block = call.at[tp, p]
        send(block, block, c_zn[p][0], h_right)
        send(block, block, c_zn[p][1], h_left)

    def c_zforward(p):
        n = plus(zh, 3 - 2 * p) * 4 + y
        block = call.at[n, p]
        arrived(block, c_zn[p][p])
        send(block, block, c_zf[p], (h_right, h_left)[p])

    def c_znear(d):
        n = plus(zh, d) * 4 + y
        way = (3 - d) // 2
        arrived(call.at[n, 1 - way], c_zn[1 - way][way])

    def c_zfar():
        n = plus(zh, 2) * 4 + y
        arrived(call.at[n, 0], c_zf[0])
        arrived(call.at[n, 1], c_zf[1])

    def c_ysend(d):
        block = call.at[plus(zh, d) * 4 + y]
        send(block, block, c_ys[d][0], y_right)
        send(block, block, c_ys[d][1], y_left)

    def c_ynear(d):
        n = plus(zh, d) * 4 + plus(y, 3)
        arrived(call.at[n], c_ys[d][0])
        send(call.at[n, 0], call.at[n, 0], c_ys[d][2], y_right)
        n = plus(zh, d) * 4 + plus(y, 1)
        arrived(call.at[n], c_ys[d][1])
        send(call.at[n, 1], call.at[n, 1], c_ys[d][3], y_left)

    def c_yfar(d):
        n = plus(zh, d) * 4 + plus(y, 2)
        arrived(call.at[n, 0], c_ys[d][2])
        arrived(call.at[n, 1], c_ys[d][3])

    def build(g16, carry):
        rows16 = filt[pl.ds(pl.multiple_of(g16 * 16, 16), 16), :].astype(F32)
        for r in range(16):
            row = jnp.concatenate([rows16[r:r + 1, :], jnp.zeros((1, 128), F32)], axis=1)
            wide = jnp.broadcast_to(row, (128, 256))
            toep[g16 * 16 + r] = pltpu.roll(wide, 0, 1, stride=1, stride_axis=0).astype(BF)
        return carry

    lane = lax.broadcasted_iota(jnp.int32, (64, 128), 1)

    def featurize(i, carry):
        rows = pl.ds(pl.multiple_of(i * 64, 64), 64)
        co = coef[rows, :]
        tl = tail_cols[rows, :]
        feats = []
        for a in range(3):
            v = inp[a, rows, :].astype(F32)
            t126, t127 = tl[:, 2 * a:2 * a + 1], tl[:, 2 * a + 1:2 * a + 2]
            v1 = jnp.where(lane == 0, t127, pltpu.roll(v, 1, 1))
            v2 = jnp.where(lane == 0, t126, jnp.where(lane == 1, t127, pltpu.roll(v, 2, 1)))
            feats.append(co[:, 3 * a:3 * a + 1] * v + co[:, 3 * a + 1:3 * a + 2] * v1 + co[:, 3 * a + 2:3 * a + 3] * v2)
        qf[rows, :] = feats[0]
        kf[rows, :] = feats[1]
        vf[rows, :] = feats[2]
        prod[rows, :] = (feats[1] * feats[2]).astype(BF)
        return carry

    def convolve(i, carry):
        pieces = []
        for j in range(8):
            rows = pl.ds(pl.multiple_of(i * 128 + j * 16, 16), 16)
            g = i * 8 + j
            cur = prod[rows, :]
            r = nn_dot(cur, toep[g, :, 0:128]) + nn_dot(prev[rows, :], toep[g, :, 128:256])
            r = r + coef[rows, 9:10] * cur.astype(F32)
            resp[rows, :] = r
            pieces.append(qf[rows, :] * r)
        columns = pl.ds(pl.multiple_of(i * 128, 128), 128)
        gated_t[core, :, columns] = jnp.concatenate(pieces, axis=0).T.astype(BF)
        return carry

    def forward(dx, steps):
        tokens = jnp.concatenate([gated_t[0], gated_t[1]], axis=0)
        for s in steps:
            n = plus(x, dx) * 4 + line[s]
            r = nn_dot(tokens, wall[n]).astype(BF)
            part[n, 0] = r[0:128, :]
            part[n, 1] = r[128:256, :]

    def backward(dx, steps, first=False):
        def one(r, carry):
            rows = pl.ds(pl.multiple_of(r * 128, 128), 128)
            total = None if first else jnp.concatenate([acc[0, rows, :], acc[1, rows, :]], axis=1)
            for s in steps:
                n = plus(x, dx) * 4 + line[s]
                term = nn_dot(wall[n, rows, :], jnp.concatenate([call[n, 0], call[n, 1]], axis=1))
                total = term if total is None else total + term
            acc[0, rows, :] = total[:, 0:128]
            acc[1, rows, :] = total[:, 128:256]
            return carry

        lax.fori_loop(0, 4, one, 0)

    zhs = [new_recv() for _ in range(2)]
    zfs = [[new_recv() for _ in range(2)] for _ in range(2)]
    zss = [new_send() for _ in range(6)]

    def y_begin(dx):
        group = plus(x, dx)
        far = group * 4 + plus(y, 2)
        send(part.at[far, 0], y_half.at[group, 0], y_sem.at[group * 4], y_right)
        send(part.at[far, 1], y_half.at[group, 1], y_sem.at[group * 4 + 1], y_left)

    def y_merge(dx):
        group = plus(x, dx)
        for way, who in ((0, y_right), (1, y_left)):
            n = group * 4 + plus(y, 1 + 2 * way)
            arrived(y_half.at[group, way], y_sem.at[group * 4 + way])
            y_stage[dx, way, way] = (part[n, way].astype(F32) + y_half[group, way].astype(F32)).astype(BF)
            y_stage[dx, way, 1 - way] = part[n, 1 - way]
            send(y_stage.at[dx, way], y_full.at[group, way], y_sem.at[group * 4 + 2 + way], who)

    z_far = [
        pltpu.make_async_remote_copy(z_stage.at[0, i], z_half.at[i], zss[i], zhs[i], device_id=who, device_id_type=MESH)
        for i, who in enumerate((h_right, h_left))
    ]
    z_near = [
        pltpu.make_async_remote_copy(
            z_stage.at[1 + way, i], z_full.at[way, i], zss[2 + 2 * way + i], zfs[way][i], device_id=who, device_id_type=MESH
        )
        for way, who in enumerate((h_right, h_left)) for i in range(2)
    ]

    def y_sum(d):
        group = plus(zh, d)
        arrived(y_full.at[group, 0], y_sem.at[group * 4 + 2])
        arrived(y_full.at[group, 1], y_sem.at[group * 4 + 3])
        return [
            part[group * 4 + y, i].astype(F32) + y_full[group, 0, i].astype(F32) + y_full[group, 1, i].astype(F32)
            for i in range(2)
        ]

    def z_first():
        sums = y_sum(2)
        for i in range(2):
            z_stage[0, i] = sums[i].astype(BF)
            z_far[i].start()

    def z_open(way):
        sums = y_sum(1 + 2 * way)
        z_stage[1 + way, 1 - way] = sums[1 - way].astype(BF)
        z_near[2 * way + 1 - way].start()
        z_mid[way] = sums[way]

    def z_second(way):
        arrived(z_half.at[way], zhs[way])
        z_stage[1 + way, way] = (z_mid[way] + z_half[way].astype(F32)).astype(BF)
        z_near[3 * way].start()

    def z_third():
        sums = y_sum(0)
        for i in range(2):
            z_own[i] = sums[i]

    turn = (
        lax.broadcasted_iota(jnp.int32, (128, 128), 0) + lax.broadcasted_iota(jnp.int32, (128, 128), 1) == 127
    ).astype(F32).astype(BF)

    def at_response(i, carry):
        rows = pl.ds(pl.multiple_of(i * 64, 64), 64)
        gg = (acc[core, rows, :] + acc_in[rows, :]).astype(BF).astype(F32)
        gout[rows, :] = (gg * qf[rows, :]).astype(BF)
        qf[rows, :] = gg * resp[rows, :]
        return carry

    def grad_product(i, carry):
        for j in range(8):
            rows = pl.ds(pl.multiple_of(i * 128 + j * 16, 16), 16)
            g = i * 8 + j
            gr = gout[rows, :]
            r = nt_dot(gr, toep[g, :, 0:128]) + nt_dot(gnext[rows, :], toep[g, :, 128:256])
            r = r + coef[rows, 9:10] * gr.astype(F32)
            k = kf[rows, :]
            kf[rows, :] = r * vf[rows, :]
            vf[rows, :] = r * k
        return carry

    def correlate(i, carry):
        base = pl.multiple_of(i * 128, 128)
        cur = nn_dot(prod[pl.ds(base, 128), :], turn).astype(BF)
        back = nn_dot(prev[pl.ds(base, 128), :], turn).astype(BF)
        sums = []
        for j in range(8):
            gr = gout[pl.ds(pl.multiple_of(i * 128 + j * 16, 16), 16), :]
            one = tn_dot(cur[16 * j:16 * (j + 1), :], gr)
            two = tn_dot(back[16 * j:16 * (j + 1), :], gr)
            both = pltpu.roll(jnp.concatenate([one, two], axis=1), 129, 1, stride=1, stride_axis=0)
            sums.append(jnp.sum(both[:, 0:128], axis=0, keepdims=True))
        pay[0, pl.ds(pl.multiple_of(i * 8, 8), 8), :] = jnp.concatenate(sums, axis=0)
        return carry

    def exchange(stage, targets):
        sems = [new_recv() for _ in targets]
        for i, who in enumerate(targets):
            send(pay.at[stage], pay_in.at[stage, i], sems[i], who)
        return sems

    def collect(stage, sems):
        total = pay[stage]
        for i, sem in enumerate(sems):
            arrived(pay_in.at[stage, i], sem)
            total = total + pay_in[stage, i]
        return total

    def short_back(i, carry):
        rows = pl.ds(pl.multiple_of(i * 64, 64), 64)
        co = coef[rows, :]
        tl = gtail_cols[rows, :]
        for a, ref in enumerate((qf, kf, vf)):
            v = ref[rows, :]
            t0, t1 = tl[:, 2 * a:2 * a + 1], tl[:, 2 * a + 1:2 * a + 2]
            v1 = jnp.where(lane == 127, t0, pltpu.roll(v, 127, 1))
            v2 = jnp.where(lane == 126, t0, jnp.where(lane == 127, t1, pltpu.roll(v, 126, 1)))
            r = co[:, 3 * a:3 * a + 1] * v + co[:, 3 * a + 1:3 * a + 2] * v1 + co[:, 3 * a + 2:3 * a + 3] * v2
            ginp[a, rows, :] = r.astype(BF)
        return carry

    w_start(0)
    r_tail = new_recv()
    send(tail_out, tail_in, r_tail, later)
    theirs = pl.ds(pl.multiple_of((1 - core) * 256, 256), 256)
    send(cot_hbm.at[theirs, :], call.at[tp, core], r_cot, sibling)

    table = jnp.concatenate([taps[0], taps[1], taps[2], skip[...], jnp.zeros((6, 512), F32)], axis=0)
    coef[...] = table.T
    arrived(tail_in, r_tail)
    tail_cols[...] = jnp.where(ctx == 0, 0.0, tail_in[...]).T
    lax.fori_loop(0, 8, featurize, 0)
    r_prod = new_recv()
    send(prod, prev, r_prod, later)
    arrived(call.at[tp, 1 - core], r_cot)
    c_zsend(0)
    c_zsend(1)
    c_ysend(0)
    lax.fori_loop(0, 2, build, 0)

    w_start(1)
    w_near(0)
    arrived(prev, r_prod)

    @pl.when(ctx == 0)
    def _():
        prev[...] = jnp.zeros((512, 128), BF)

    lax.fori_loop(0, 4, convolve, 0)
    r_gated = new_recv()
    send(gated_t.at[core], gated_t.at[core], r_gated, sibling)
    w_start(2)
    c_ynear(0)
    w_near(1)
    c_zforward(0)
    c_zforward(1)
    c_znear(3)
    c_znear(1)
    c_ysend(3)
    c_ysend(1)
    arrived(gated_t.at[1 - core], r_gated)
    w_start(3)
    w_far(0)
    forward(0, (0, 1, 2, 3))
    y_begin(0)
    for d in (3, 1, 2):
        forward(d, (0,))
    c_zfar()
    c_ysend(2)
    w_near(2)
    c_yfar(0)
    c_ynear(3)
    c_ynear(1)
    w_far(1)
    for d in (3, 1, 2):
        forward(d, (1,))
    y_merge(0)
    w_near(3)
    forward(3, (2, 3))
    y_begin(3)
    forward(1, (2, 3))
    y_begin(1)
    w_far(2)
    forward(2, (2,))
    w_far(3)
    forward(2, (3,))
    y_begin(2)
    c_ynear(2)
    y_merge(3)
    y_merge(1)
    y_merge(2)
    c_yfar(3)
    c_yfar(1)
    c_yfar(2)
    backward(0, (0, 1, 2, 3), True)
    backward(3, (0, 1, 2, 3))
    backward(1, (0, 1, 2, 3))
    backward(2, (0, 1, 2, 3))
    r_acc = new_recv()
    send(acc.at[1 - core], acc_in, r_acc, sibling)
    z_first()
    z_open(0)
    z_open(1)
    arrived(acc_in, r_acc)
    lax.fori_loop(0, 8, at_response, 0)
    r_gout = new_recv()
    send(gout, gnext, r_gout, earlier)
    lax.fori_loop(0, 4, correlate, 0)
    for i in range(4):
        both = gout[128 * i:128 * (i + 1), :].astype(F32) * prod[128 * i:128 * (i + 1), :].astype(F32)
        pay[0, 32 + i:33 + i, :] = jnp.sum(both.T, axis=0, keepdims=True)
    pay[0, 36:40, :] = jnp.zeros((4, 128), F32)
    px = exchange(0, [x_right, x_left, x_far])
    arrived(gnext, r_gout)

    @pl.when(ctx == 31)
    def _():
        gnext[...] = jnp.zeros((512, 128), BF)

    lax.fori_loop(0, 4, grad_product, 0)
    for a, ref in enumerate((qf, kf, vf)):
        gtail_out[2 * a:2 * a + 2, :] = ref[:, 0:128].T[0:2, :]
    gtail_out[6:8, :] = jnp.zeros((2, 512), F32)
    r_gtail = new_recv()
    send(gtail_out, gtail_in, r_gtail, earlier)
    z_second(0)
    z_second(1)
    z_third()
    pay[1] = collect(0, px)
    pz = exchange(1, [l_up, l_down, l_far])

    arrived(gtail_in, r_gtail)
    gtail_cols[...] = jnp.where(ctx == 31, 0.0, gtail_in[...]).T
    lax.fori_loop(0, 8, short_back, 0)
    pay[2] = collect(1, pz)
    pc = exchange(2, [sibling])

    for way in range(2):
        for i in range(2):
            arrived(z_full.at[way, i], zfs[way][i])
    fin[...] = z_own[...] + z_full[0].astype(F32) + z_full[1].astype(F32)
    fin_out[...] = fin[1 - core].astype(BF)
    r_fin = new_recv()
    send(fin_out, fin_in, r_fin, sibling)
    out[pl.ds(pl.multiple_of(core * 256, 256), 256), :] = fin[core].T.astype(BF)
    total = collect(2, pc)
    gfilt[...] = total[0:32, :]
    gskip[...] = total[32:40, :]
    arrived(fin_in, r_fin)
    out[theirs, :] = fin_in[...].astype(F32).T.astype(BF)

    for copy, when in sends:
        if when is None:
            copy.wait_send()
        else:
            pl.when(when)(lambda copy=copy: copy.wait_send())
    for copy in z_far + z_near:
        copy.wait_send()
    assert count["s"] <= N_SEND and count["r"] <= N_RECV


def body(inputs, short_filters, explicit_filter, skip_gain, out_weight, out_cotangent):
    vmem = pl.BlockSpec(memory_space=pltpu.VMEM)
    hbm = pl.BlockSpec(memory_space=pltpu.HBM)
    out, ginp, gfilt, gskip = pl.pallas_call(
        kernel,
        out_shape=(
            jax.ShapeDtypeStruct((512, 128), BF),
            jax.ShapeDtypeStruct((3, 512, 128), BF),
            jax.ShapeDtypeStruct((32, 128), F32),
            jax.ShapeDtypeStruct((8, 128), F32),
        ),
        in_specs=[hbm] * 6,
        out_specs=(vmem, vmem, vmem, vmem),
        scratch_shapes=[
            pltpu.VMEM((3, 512, 128), BF),
            pltpu.VMEM((3, 3, 512), F32),
            pltpu.VMEM((32, 128), BF),
            pltpu.VMEM((1, 512), F32),
            pltpu.VMEM((16, 512, 256), BF),
            pltpu.VMEM((16, 2, 256, 128), BF),
            pltpu.VMEM((32, 128, 256), BF),
            pltpu.VMEM((512, 16), F32),
            pltpu.VMEM((8, 512), F32),
            pltpu.VMEM((8, 512), F32),
            pltpu.VMEM((512, 8), F32),
            pltpu.VMEM((512, 128), F32),
            pltpu.VMEM((512, 128), F32),
            pltpu.VMEM((512, 128), F32),
            pltpu.VMEM((512, 128), BF),
            pltpu.VMEM((512, 128), BF),
            pltpu.VMEM((512, 128), F32),
            pltpu.VMEM((2, 128, 512), BF),
            pltpu.VMEM((2, 512, 128), F32),
            pltpu.VMEM((512, 128), F32),
            pltpu.VMEM((16, 2, 128, 256), BF),
            pltpu.VMEM((512, 128), BF),
            pltpu.VMEM((512, 128), BF),
            pltpu.VMEM((8, 512), F32),
            pltpu.VMEM((8, 512), F32),
            pltpu.VMEM((512, 8), F32),
            pltpu.VMEM((4, 2, 128, 256), BF),
            pltpu.VMEM((4, 2, 2, 128, 256), BF),
            pltpu.VMEM((4, 2, 2, 128, 256), BF),
            pltpu.VMEM((2, 128, 256), BF),
            pltpu.VMEM((2, 2, 128, 256), BF),
            pltpu.VMEM((3, 2, 128, 256), BF),
            pltpu.VMEM((2, 128, 256), F32),
            pltpu.VMEM((2, 128, 256), F32),
            pltpu.VMEM((2, 128, 256), F32),
            pltpu.VMEM((128, 256), BF),
            pltpu.VMEM((128, 256), BF),
            pltpu.VMEM((3, 40, 128), F32),
            pltpu.VMEM((3, 3, 40, 128), F32),
            pltpu.SemaphoreType.DMA((6,)),
            pltpu.SemaphoreType.DMA((N_SEND,)),
            pltpu.SemaphoreType.DMA((N_RECV,)),
            pltpu.SemaphoreType.DMA((4,)),
            pltpu.SemaphoreType.DMA((16,)),
        ],
        compiler_params=pltpu.CompilerParams(
            collective_id=0, has_side_effects=True, vmem_limit_bytes=60 * 1024 * 1024
        ),
        cost_estimate=pl.CostEstimate(flops=2600000000, bytes_accessed=4000000, transcendentals=0),
    )(inputs, short_filters, explicit_filter, skip_gain.reshape(1, 512), out_weight, out_cotangent)
    return (out, ginp, gfilt, gskip[0:4].reshape(512))


def solution(mesh):
    placed = (
        P(None, "tp", "ctx"),
        P(None, None, "tp"),
        P("tp", None),
        P("tp"),
        P("tp", "ctx"),
        P("tp", "ctx"),
    )
    return jax.shard_map(
        body,
        mesh=mesh,
        in_specs=placed,
        out_specs=(P("tp", "ctx"), P(None, "tp", "ctx"), P("tp", None), P("tp")),
        check_vma=False,
    )
```

```python
import jax
import jax.numpy as jnp
from jax import lax
from jax.experimental import pallas as pl
from jax.experimental.pallas import tpu as pltpu
from jax.sharding import PartitionSpec as P

MESH = pl.DeviceIdType.MESH
BF = jnp.bfloat16
F32 = jnp.float32
N_SEND = 128
N_RECV = 128


def nt_dot(a, b):
    return lax.dot_general(a, b, (((1,), (1,)), ((), ())), preferred_element_type=F32)


def tn_dot(a, b):
    return lax.dot_general(a, b, (((0,), (0,)), ((), ())), preferred_element_type=F32)


def nn_dot(a, b):
    return jnp.dot(a, b, preferred_element_type=F32)


def kernel(
    inp_hbm, taps_hbm, filt_hbm, skip_hbm, w_hbm, cot_hbm,
    out, ginp, gsums,
    inp, taps, filt, skip, wall, call, toep, coef, tail_out, tail_in, tail_cols, qf, kf, vf, prod, prev, resp, gated_t,
    acc, acc_in, part, gout, gnext, gtail_out, gtail_in, gtail_cols,
    y_half, y_full, y_stage, z_half, z_full, z_stage, z_own, z_mid, fin, fin_out, fin_in,
    pay, pay_in, local_sem, ssem, rsem, wz_sem, y_sem,
):
    ctx, tp = lax.axis_index("ctx"), lax.axis_index("tp")
    x, zl, core = ctx // 8, (ctx // 2) % 4, ctx % 2
    zh, y = tp // 4, tp % 4
    own = x * 4 + zl

    local = [
        pltpu.make_async_copy(w_hbm, wall.at[own], local_sem.at[0]),
        pltpu.make_async_copy(inp_hbm, inp, local_sem.at[1]),
        pltpu.make_async_copy(taps_hbm, taps, local_sem.at[2]),
        pltpu.make_async_copy(skip_hbm, skip, local_sem.at[3]),
        pltpu.make_async_copy(filt_hbm, filt, local_sem.at[4]),
        pltpu.make_async_copy(cot_hbm.at[pl.ds(pl.multiple_of(core * 256, 256), 256), :], call.at[tp, core], local_sem.at[5]),
    ]
    for copy in local:
        copy.start()

    def at_ctx(x_, zl_, core_):
        return ((x_ * 4 + zl_) * 2 + core_, tp)

    def at_tp(zh_, y_):
        return (ctx, zh_ * 4 + y_)

    def plus(v, d):
        return (v + d) % 4

    x_right, x_left, x_far = at_ctx(plus(x, 1), zl, core), at_ctx(plus(x, 3), zl, core), at_ctx(plus(x, 2), zl, core)
    l_up, l_down, l_far = at_ctx(x, plus(zl, 1), core), at_ctx(x, plus(zl, 3), core), at_ctx(x, plus(zl, 2), core)
    sibling = at_ctx(x, zl, 1 - core)
    later, earlier = ((ctx + 1) % 32, tp), ((ctx + 31) % 32, tp)
    h_right, h_left = at_tp(plus(zh, 1), y), at_tp(plus(zh, 3), y)
    y_right, y_left = at_tp(zh, plus(y, 1)), at_tp(zh, plus(y, 3))

    upper = zl // 2
    inner = zl + upper * (3 - 2 * zl)
    step_dir = 1 - 2 * upper
    z_in = at_ctx(x, zl + step_dir, core)
    z_out = at_ctx(x, (zl - step_dir + 4) % 4, core)

    def unmirror(v):
        return v + upper * (3 - 2 * v)

    line = [zl, unmirror(1 - inner), unmirror(2), unmirror(3)]

    partners = [x_right, x_left, x_far, l_up, l_down, l_far, sibling, later, earlier, h_right, h_left, y_right, y_left]
    barrier = pltpu.get_barrier_semaphore()
    for who in partners:
        pl.semaphore_signal(barrier, inc=1, device_id=who, device_id_type=MESH)

    count = {"s": 0, "r": 0}
    sends = []

    def new_recv():
        count["r"] += 1
        return rsem.at[count["r"] - 1]

    def new_send():
        count["s"] += 1
        return ssem.at[count["s"] - 1]

    def send(src, dst, sem, who, when=None):
        copy = pltpu.make_async_remote_copy(src, dst, new_send(), sem, device_id=who, device_id_type=MESH)
        if when is None:
            copy.start()
        else:
            pl.when(when)(lambda: copy.start())
        sends.append((copy, when))

    def arrived(dst, sem):
        pltpu.make_async_remote_copy(dst, dst, ssem.at[0], sem, device_id=sibling, device_id_type=MESH).wait_recv()

    local[1].wait()
    for a in range(3):
        turned = inp[a].astype(F32).T
        tail_out[2 * a:2 * a + 2, :] = turned[126:128, :]
    tail_out[6:8, :] = jnp.zeros((2, 512), F32)
    for copy in (local[2], local[3], local[4], local[5], local[0]):
        copy.wait()
    pl.semaphore_wait(barrier, len(partners))

    x_sems = [[new_recv() for _ in range(4)] for _ in range(4)]
    lo, hi = pl.ds(0, 256), pl.ds(256, 256)

    def w_start(s):
        n = x * 4 + line[s]
        block = wall.at[n]
        if s > 0:
            arrived(block, wz_sem.at[line[s]])
        if s == 0:
            send(block, block, wz_sem.at[line[s]], z_in)
            send(block, block, wz_sem.at[line[s]], z_out, inner == 1)
        elif s == 1:
            send(block, block, wz_sem.at[line[s]], z_in, inner == 1)
        else:
            send(block, block, wz_sem.at[line[s]], z_out, inner == 1)
        send(block, block, x_sems[s][0], x_right)
        send(block, block, x_sems[s][1], x_left)

    def w_near(s):
        n = plus(x, 3) * 4 + line[s]
        arrived(wall.at[n], x_sems[s][0])
        half = wall.at[n, lo, :]
        send(half, half, x_sems[s][2], x_right)
        n = plus(x, 1) * 4 + line[s]
        arrived(wall.at[n], x_sems[s][1])
        half = wall.at[n, hi, :]
        send(half, half, x_sems[s][3], x_left)

    def w_far(s):
        n = plus(x, 2) * 4 + line[s]
        arrived(wall.at[n, lo, :], x_sems[s][2])
        arrived(wall.at[n, hi, :], x_sems[s][3])

    r_cot = new_recv()
    c_zn = [[new_recv() for _ in range(2)] for _ in range(2)]
    c_zf = [new_recv() for _ in range(2)]
    c_ys = [[new_recv() for _ in range(4)] for _ in range(4)]

    def c_zsend(p):
        block = call.at[tp, p]
        send(block, block, c_zn[p][0], h_right)
        send(block, block, c_zn[p][1], h_left)

    def c_zforward(p):
        n = plus(zh, 3 - 2 * p) * 4 + y
        block = call.at[n, p]
        arrived(block, c_zn[p][p])
        send(block, block, c_zf[p], (h_right, h_left)[p])

    def c_znear(d):
        n = plus(zh, d) * 4 + y
        way = (3 - d) // 2
        arrived(call.at[n, 1 - way], c_zn[1 - way][way])

    def c_zfar():
        n = plus(zh, 2) * 4 + y
        arrived(call.at[n, 0], c_zf[0])
        arrived(call.at[n, 1], c_zf[1])

    def c_ysend(d):
        block = call.at[plus(zh, d) * 4 + y]
        send(block, block, c_ys[d][0], y_right)
        send(block, block, c_ys[d][1], y_left)

    def c_ynear(d):
        n = plus(zh, d) * 4 + plus(y, 3)
        arrived(call.at[n], c_ys[d][0])
        send(call.at[n, 0], call.at[n, 0], c_ys[d][2], y_right)
        n = plus(zh, d) * 4 + plus(y, 1)
        arrived(call.at[n], c_ys[d][1])
        send(call.at[n, 1], call.at[n, 1], c_ys[d][3], y_left)

    def c_yfar(d):
        n = plus(zh, d) * 4 + plus(y, 2)
        arrived(call.at[n, 0], c_ys[d][2])
        arrived(call.at[n, 1], c_ys[d][3])

    def build(g16, carry):
        rows16 = filt[pl.ds(pl.multiple_of(g16 * 16, 16), 16), :].astype(F32)
        for r in range(16):
            row = jnp.concatenate([rows16[r:r + 1, :], jnp.zeros((1, 128), F32)], axis=1)
            wide = jnp.broadcast_to(row, (128, 256))
            toep[g16 * 16 + r] = pltpu.roll(wide, 0, 1, stride=1, stride_axis=0).astype(BF)
        return carry

    lane = lax.broadcasted_iota(jnp.int32, (64, 128), 1)

    def featurize(i, carry):
        rows = pl.ds(pl.multiple_of(i * 64, 64), 64)
        co = coef[rows, :]
        tl = tail_cols[rows, :]
        feats = []
        for a in range(3):
            v = inp[a, rows, :].astype(F32)
            t126, t127 = tl[:, 2 * a:2 * a + 1], tl[:, 2 * a + 1:2 * a + 2]
            v1 = jnp.where(lane == 0, t127, pltpu.roll(v, 1, 1))
            v2 = jnp.where(lane == 0, t126, jnp.where(lane == 1, t127, pltpu.roll(v, 2, 1)))
            feats.append(co[:, 3 * a:3 * a + 1] * v + co[:, 3 * a + 1:3 * a + 2] * v1 + co[:, 3 * a + 2:3 * a + 3] * v2)
        qf[rows, :] = feats[0]
        kf[rows, :] = feats[1]
        vf[rows, :] = feats[2]
        prod[rows, :] = (feats[1] * feats[2]).astype(BF)
        return carry

    def convolve(i, carry):
        pieces = []
        for j in range(8):
            rows = pl.ds(pl.multiple_of(i * 128 + j * 16, 16), 16)
            g = i * 8 + j
            cur = prod[rows, :]
            r = nn_dot(cur, toep[g, :, 0:128]) + nn_dot(prev[rows, :], toep[g, :, 128:256])
            r = r + coef[rows, 9:10] * cur.astype(F32)
            resp[rows, :] = r
            pieces.append(qf[rows, :] * r)
        columns = pl.ds(pl.multiple_of(i * 128, 128), 128)
        gated_t[core, :, columns] = jnp.concatenate(pieces, axis=0).T.astype(BF)
        return carry

    def forward(dx, steps):
        tokens = jnp.concatenate([gated_t[0], gated_t[1]], axis=0)
        for s in steps:
            n = plus(x, dx) * 4 + line[s]
            r = nn_dot(tokens, wall[n]).astype(BF)
            part[n, 0] = r[0:128, :]
            part[n, 1] = r[128:256, :]

    def backward(dx, steps, first=False):
        def one(r, carry):
            rows = pl.ds(pl.multiple_of(r * 128, 128), 128)
            total = None if first else jnp.concatenate([acc[0, rows, :], acc[1, rows, :]], axis=1)
            for s in steps:
                n = plus(x, dx) * 4 + line[s]
                term = nn_dot(wall[n, rows, :], jnp.concatenate([call[n, 0], call[n, 1]], axis=1))
                total = term if total is None else total + term
            acc[0, rows, :] = total[:, 0:128]
            acc[1, rows, :] = total[:, 128:256]
            return carry

        lax.fori_loop(0, 4, one, 0)

    zhs = [new_recv() for _ in range(2)]
    zfs = [[new_recv() for _ in range(2)] for _ in range(2)]
    zss = [new_send() for _ in range(6)]

    def y_begin(dx):
        group = plus(x, dx)
        far = group * 4 + plus(y, 2)
        send(part.at[far, 0], y_half.at[group, 0], y_sem.at[group * 4], y_right)
        send(part.at[far, 1], y_half.at[group, 1], y_sem.at[group * 4 + 1], y_left)

    def y_merge(dx):
        group = plus(x, dx)
        for way, who in ((0, y_right), (1, y_left)):
            n = group * 4 + plus(y, 1 + 2 * way)
            arrived(y_half.at[group, way], y_sem.at[group * 4 + way])
            y_stage[dx, way, way] = (part[n, way].astype(F32) + y_half[group, way].astype(F32)).astype(BF)
            y_stage[dx, way, 1 - way] = part[n, 1 - way]
            send(y_stage.at[dx, way], y_full.at[group, way], y_sem.at[group * 4 + 2 + way], who)

    z_far = [
        pltpu.make_async_remote_copy(z_stage.at[0, i], z_half.at[i], zss[i], zhs[i], device_id=who, device_id_type=MESH)
        for i, who in enumerate((h_right, h_left))
    ]
    z_near = [
        pltpu.make_async_remote_copy(
            z_stage.at[1 + way, i], z_full.at[way, i], zss[2 + 2 * way + i], zfs[way][i], device_id=who, device_id_type=MESH
        )
        for way, who in enumerate((h_right, h_left)) for i in range(2)
    ]

    def y_sum(d):
        group = plus(zh, d)
        arrived(y_full.at[group, 0], y_sem.at[group * 4 + 2])
        arrived(y_full.at[group, 1], y_sem.at[group * 4 + 3])
        return [
            part[group * 4 + y, i].astype(F32) + y_full[group, 0, i].astype(F32) + y_full[group, 1, i].astype(F32)
            for i in range(2)
        ]

    def z_first():
        sums = y_sum(2)
        for i in range(2):
            z_stage[0, i] = sums[i].astype(BF)
            z_far[i].start()

    def z_open(way):
        sums = y_sum(1 + 2 * way)
        z_stage[1 + way, 1 - way] = sums[1 - way].astype(BF)
        z_near[2 * way + 1 - way].start()
        z_mid[way] = sums[way]

    def z_second(way):
        arrived(z_half.at[way], zhs[way])
        z_stage[1 + way, way] = (z_mid[way] + z_half[way].astype(F32)).astype(BF)
        z_near[3 * way].start()

    def z_third():
        sums = y_sum(0)
        for i in range(2):
            z_own[i] = sums[i]

    turn = (
        lax.broadcasted_iota(jnp.int32, (128, 128), 0) + lax.broadcasted_iota(jnp.int32, (128, 128), 1) == 127
    ).astype(F32).astype(BF)

    def at_response(i, carry):
        rows = pl.ds(pl.multiple_of(i * 64, 64), 64)
        gg = (acc[core, rows, :] + acc_in[rows, :]).astype(BF).astype(F32)
        gout[rows, :] = (gg * qf[rows, :]).astype(BF)
        qf[rows, :] = gg * resp[rows, :]
        return carry

    def grad_product(i, carry):
        for j in range(8):
            rows = pl.ds(pl.multiple_of(i * 128 + j * 16, 16), 16)
            g = i * 8 + j
            gr = gout[rows, :]
            r = nt_dot(gr, toep[g, :, 0:128]) + nt_dot(gnext[rows, :], toep[g, :, 128:256])
            r = r + coef[rows, 9:10] * gr.astype(F32)
            k = kf[rows, :]
            kf[rows, :] = r * vf[rows, :]
            vf[rows, :] = r * k
        return carry

    def correlate(i, carry):
        base = pl.multiple_of(i * 128, 128)
        cur = nn_dot(prod[pl.ds(base, 128), :], turn).astype(BF)
        back = nn_dot(prev[pl.ds(base, 128), :], turn).astype(BF)
        sums = []
        for j in range(8):
            gr = gout[pl.ds(pl.multiple_of(i * 128 + j * 16, 16), 16), :]
            one = tn_dot(cur[16 * j:16 * (j + 1), :], gr)
            two = tn_dot(back[16 * j:16 * (j + 1), :], gr)
            both = pltpu.roll(jnp.concatenate([one, two], axis=1), 129, 1, stride=1, stride_axis=0)
            sums.append(jnp.sum(both[:, 0:128], axis=0, keepdims=True))
        pay[0, pl.ds(pl.multiple_of(i * 8, 8), 8), :] = jnp.concatenate(sums, axis=0)
        return carry

    def exchange(stage, targets):
        sems = [new_recv() for _ in targets]
        for i, who in enumerate(targets):
            send(pay.at[stage], pay_in.at[stage, i], sems[i], who)
        return sems

    def collect(stage, sems):
        total = pay[stage]
        for i, sem in enumerate(sems):
            arrived(pay_in.at[stage, i], sem)
            total = total + pay_in[stage, i]
        return total

    def short_back(i, carry):
        rows = pl.ds(pl.multiple_of(i * 64, 64), 64)
        co = coef[rows, :]
        tl = gtail_cols[rows, :]
        for a, ref in enumerate((qf, kf, vf)):
            v = ref[rows, :]
            t0, t1 = tl[:, 2 * a:2 * a + 1], tl[:, 2 * a + 1:2 * a + 2]
            v1 = jnp.where(lane == 127, t0, pltpu.roll(v, 127, 1))
            v2 = jnp.where(lane == 126, t0, jnp.where(lane == 127, t1, pltpu.roll(v, 126, 1)))
            r = co[:, 3 * a:3 * a + 1] * v + co[:, 3 * a + 1:3 * a + 2] * v1 + co[:, 3 * a + 2:3 * a + 3] * v2
            ginp[a, rows, :] = r.astype(BF)
        return carry

    w_start(0)
    r_tail = new_recv()
    send(tail_out, tail_in, r_tail, later)
    theirs = pl.ds(pl.multiple_of((1 - core) * 256, 256), 256)
    send(cot_hbm.at[theirs, :], call.at[tp, core], r_cot, sibling)

    table = jnp.concatenate([taps[0], taps[1], taps[2], skip[...], jnp.zeros((6, 512), F32)], axis=0)
    coef[...] = table.T
    arrived(tail_in, r_tail)
    tail_cols[...] = jnp.where(ctx == 0, 0.0, tail_in[...]).T
    lax.fori_loop(0, 8, featurize, 0)
    r_prod = new_recv()
    send(prod, prev, r_prod, later)
    arrived(call.at[tp, 1 - core], r_cot)
    c_zsend(0)
    c_zsend(1)
    c_ysend(0)
    lax.fori_loop(0, 2, build, 0)

    w_start(1)
    w_near(0)
    arrived(prev, r_prod)

    @pl.when(ctx == 0)
    def _():
        prev[...] = jnp.zeros((512, 128), BF)

    lax.fori_loop(0, 4, convolve, 0)
    r_gated = new_recv()
    send(gated_t.at[core], gated_t.at[core], r_gated, sibling)
    w_start(2)
    c_ynear(0)
    w_near(1)
    c_zforward(0)
    c_zforward(1)
    c_znear(3)
    c_znear(1)
    c_ysend(3)
    c_ysend(1)
    arrived(gated_t.at[1 - core], r_gated)
    w_start(3)
    w_far(0)
    forward(0, (0, 1, 2, 3))
    y_begin(0)
    for d in (3, 1, 2):
        forward(d, (0,))
    c_zfar()
    c_ysend(2)
    w_near(2)
    c_yfar(0)
    c_ynear(3)
    c_ynear(1)
    w_far(1)
    for d in (3, 1, 2):
        forward(d, (1,))
    y_merge(0)
    w_near(3)
    forward(3, (2, 3))
    y_begin(3)
    forward(1, (2, 3))
    y_begin(1)
    w_far(2)
    forward(2, (2,))
    w_far(3)
    forward(2, (3,))
    y_begin(2)
    c_ynear(2)
    y_merge(3)
    y_merge(1)
    y_merge(2)
    c_yfar(3)
    c_yfar(1)
    c_yfar(2)
    backward(0, (0, 1, 2, 3), True)
    backward(3, (0, 1, 2, 3))
    backward(1, (0, 1, 2, 3))
    backward(2, (0, 1, 2, 3))
    r_acc = new_recv()
    send(acc.at[1 - core], acc_in, r_acc, sibling)
    z_first()
    z_open(0)
    z_open(1)
    arrived(acc_in, r_acc)
    lax.fori_loop(0, 8, at_response, 0)
    r_gout = new_recv()
    send(gout, gnext, r_gout, earlier)
    lax.fori_loop(0, 4, correlate, 0)
    for i in range(4):
        both = gout[128 * i:128 * (i + 1), :].astype(F32) * prod[128 * i:128 * (i + 1), :].astype(F32)
        pay[0, 32 + i:33 + i, :] = jnp.sum(both.T, axis=0, keepdims=True)
    pay[0, 36:40, :] = jnp.zeros((4, 128), F32)
    px = exchange(0, [x_right, x_left, x_far])
    arrived(gnext, r_gout)

    @pl.when(ctx == 31)
    def _():
        gnext[...] = jnp.zeros((512, 128), BF)

    lax.fori_loop(0, 4, grad_product, 0)
    for a, ref in enumerate((qf, kf, vf)):
        gtail_out[2 * a:2 * a + 2, :] = ref[:, 0:128].T[0:2, :]
    gtail_out[6:8, :] = jnp.zeros((2, 512), F32)
    r_gtail = new_recv()
    send(gtail_out, gtail_in, r_gtail, earlier)
    z_second(0)
    z_second(1)
    z_third()
    pay[1] = collect(0, px)
    pz = exchange(1, [l_up, l_down, l_far])

    arrived(gtail_in, r_gtail)
    gtail_cols[...] = jnp.where(ctx == 31, 0.0, gtail_in[...]).T
    lax.fori_loop(0, 8, short_back, 0)
    pay[2] = collect(1, pz)
    pc = exchange(2, [sibling])

    for way in range(2):
        for i in range(2):
            arrived(z_full.at[way, i], zfs[way][i])
    fin[...] = z_own[...] + z_full[0].astype(F32) + z_full[1].astype(F32)
    fin_out[...] = fin[1 - core].astype(BF)
    r_fin = new_recv()
    send(fin_out, fin_in, r_fin, sibling)
    out[pl.ds(pl.multiple_of(core * 256, 256), 256), :] = fin[core].T.astype(BF)
    gsums[...] = collect(2, pc)
    arrived(fin_in, r_fin)
    out[theirs, :] = fin_in[...].astype(F32).T.astype(BF)

    for copy, when in sends:
        if when is None:
            copy.wait_send()
        else:
            pl.when(when)(lambda copy=copy: copy.wait_send())
    for copy in z_far + z_near:
        copy.wait_send()
    assert count["s"] <= N_SEND and count["r"] <= N_RECV


def body(inputs, short_filters, explicit_filter, skip_gain, out_weight, out_cotangent):
    vmem = pl.BlockSpec(memory_space=pltpu.VMEM)
    hbm = pl.BlockSpec(memory_space=pltpu.HBM)
    out, ginp, gsums = pl.pallas_call(
        kernel,
        out_shape=(
            jax.ShapeDtypeStruct((512, 128), BF),
            jax.ShapeDtypeStruct((3, 512, 128), BF),
            jax.ShapeDtypeStruct((40, 128), F32),
        ),
        in_specs=[hbm] * 6,
        out_specs=(vmem, vmem, vmem),
        scratch_shapes=[
            pltpu.VMEM((3, 512, 128), BF),
            pltpu.VMEM((3, 3, 512), F32),
            pltpu.VMEM((32, 128), BF),
            pltpu.VMEM((1, 512), F32),
            pltpu.VMEM((16, 512, 256), BF),
            pltpu.VMEM((16, 2, 256, 128), BF),
            pltpu.VMEM((32, 128, 256), BF),
            pltpu.VMEM((512, 16), F32),
            pltpu.VMEM((8, 512), F32),
            pltpu.VMEM((8, 512), F32),
            pltpu.VMEM((512, 8), F32),
            pltpu.VMEM((512, 128), F32),
            pltpu.VMEM((512, 128), F32),
            pltpu.VMEM((512, 128), F32),
            pltpu.VMEM((512, 128), BF),
            pltpu.VMEM((512, 128), BF),
            pltpu.VMEM((512, 128), F32),
            pltpu.VMEM((2, 128, 512), BF),
            pltpu.VMEM((2, 512, 128), F32),
            pltpu.VMEM((512, 128), F32),
            pltpu.VMEM((16, 2, 128, 256), BF),
            pltpu.VMEM((512, 128), BF),
            pltpu.VMEM((512, 128), BF),
            pltpu.VMEM((8, 512), F32),
            pltpu.VMEM((8, 512), F32),
            pltpu.VMEM((512, 8), F32),
            pltpu.VMEM((4, 2, 128, 256), BF),
            pltpu.VMEM((4, 2, 2, 128, 256), BF),
            pltpu.VMEM((4, 2, 2, 128, 256), BF),
            pltpu.VMEM((2, 128, 256), BF),
            pltpu.VMEM((2, 2, 128, 256), BF),
            pltpu.VMEM((3, 2, 128, 256), BF),
            pltpu.VMEM((2, 128, 256), F32),
            pltpu.VMEM((2, 128, 256), F32),
            pltpu.VMEM((2, 128, 256), F32),
            pltpu.VMEM((128, 256), BF),
            pltpu.VMEM((128, 256), BF),
            pltpu.VMEM((3, 40, 128), F32),
            pltpu.VMEM((3, 3, 40, 128), F32),
            pltpu.SemaphoreType.DMA((6,)),
            pltpu.SemaphoreType.DMA((N_SEND,)),
            pltpu.SemaphoreType.DMA((N_RECV,)),
            pltpu.SemaphoreType.DMA((4,)),
            pltpu.SemaphoreType.DMA((16,)),
        ],
        compiler_params=pltpu.CompilerParams(
            collective_id=0, has_side_effects=True, vmem_limit_bytes=60 * 1024 * 1024
        ),
        cost_estimate=pl.CostEstimate(flops=2600000000, bytes_accessed=4000000, transcendentals=0),
    )(inputs, short_filters, explicit_filter, skip_gain.reshape(1, 512), out_weight, out_cotangent)
    return (out, ginp, gsums[0:32], gsums[32:36].reshape(512))


def solution(mesh):
    placed = (
        P(None, "tp", "ctx"),
        P(None, None, "tp"),
        P("tp", None),
        P("tp"),
        P("tp", "ctx"),
        P("tp", "ctx"),
    )
    return jax.shard_map(
        body,
        mesh=mesh,
        in_specs=placed,
        out_specs=(P("tp", "ctx"), P(None, "tp", "ctx"), P("tp", None), P("tp")),
        check_vma=False,
    )
```
